256 devices in a mesh: expert: 16 (over z, core), tensor: 16 (over y, x).
Axes of the slice: x: 4, y: 4, z: 8, core: 2. Of those that a mesh axis runs over, the one named last changes fastest.
Arguments:
- tokens: bfloat16 [32768, 4096], P(('expert', 'tensor')), may hold values from -6 to 6
- cotangent: bfloat16 [32768, 4096], P(('expert', 'tensor')), may hold values from -6 to 6
- expert_ids: int32 [32768, 1], P(('expert', 'tensor')), may hold values from 0 to 63; in each aligned block of 128 rows (0 to 127, 128 to 255, ...) at most 3 rows name the same one
- gate_values: bfloat16 [32768, 1], P(('expert', 'tensor')), may hold values from 0.049804688 to 0.5
- gate_weight: bfloat16 [256, 384, 4096], P(('expert', 'tensor')), may hold values from -0.09375 to 0.09375
- up_weight: bfloat16 [256, 384, 4096], P(('expert', 'tensor')), may hold values from -0.09375 to 0.09375
- down_weight: bfloat16 [256, 384, 4096], P(('expert', 'tensor')), may hold values from -0.15625 to 0.15625
Outputs:
- d_tokens: bfloat16 [32768, 4096], P(('expert', 'tensor'))
- gate_grad: bfloat16 [32768, 1], P(('expert', 'tensor'))
The draws below stay inside these ranges and needn't reach their ends.
Inputs may be any that keep to these rules, and one draw needn't show every extreme that they name: `expert_ids`: each row names one expert. Among the rows of one device (aligned blocks of 128 tokens) no expert is named more than 3 times, a bound that some block reaches.
All inputs are finite; a program needn't handle non-finite values.
Results may differ from the reference program's by a relative error of at most 0.02.
Values may be sent and summed in bfloat16 or wider, within the bound.
A program may use at most 128 MiB of HBM per device.

```python
import math
import jax
import jax.numpy as jnp
import numpy as np
from jax import lax

D = 4096
FF = 1536
TOP = 1
SPLIT = 4
TOK_DEV = 128
EXPERTS = 64
TOKENS = 32768
CAP = 3
HID = 384
N_EXPERT = 16
N_TENSOR = 16


def block_scale(stream_key, dims, shards, smallest, top_value):
    loudness, own = 1.0, jax.random.fold_in(stream_key, 6)
    for axis_at, parts in shards:
        steps = jnp.exp(jax.random.uniform(jax.random.fold_in(own, axis_at), (parts,), jnp.float32, smallest / len(shards), top_value / len(shards)))
        loudness = loudness * jnp.repeat(steps, dims[axis_at] // parts).reshape([-1 if axis == axis_at else 1 for axis in range(len(dims))])
    return loudness


def shared_out(rng, own, number, rows, amount, top, limit, lean):
    sequence = jax.random.permutation(rng, amount)
    packed, usual = load_shares(amount, rows * top, limit, lean, True), load_shares(amount, rows * top, limit, lean, False)
    places = jnp.arange(amount)

    def named(tallies, rotation):
        used = int((tallies > 0).sum())
        fixed = max(1, used // 4)
        passed = fixed + (places - fixed + rotation * (used - fixed)) % max(1, amount - fixed)
        return jnp.zeros((amount,), jnp.int32).at[sequence[jnp.where(places < fixed, places, passed)]].set(jnp.asarray(tallies, jnp.int32))

    tallies = jnp.where(number % 4 == 0, named(packed, number // 4), named(usual, number - number // 4 - 1))
    mixed = jax.random.permutation(jax.random.fold_in(own, 3), amount)
    source_of, sink = mixed[0:amount // 2 * 2:2], mixed[1:amount // 2 * 2:2]
    margin = jnp.minimum(tallies[source_of] - 1, limit - tallies[sink]) // 2
    margin = jnp.where((source_of == sequence[0]) | (sink == sequence[0]) | (tallies[sink] == 0), 0, jnp.maximum(margin, 0))
    passed = jax.random.randint(jax.random.fold_in(own, 4), (amount // 2,), 0, 1 << 20) % (margin + 1)
    tallies = tallies.at[source_of].add(-passed).at[sink].add(passed)
    items = jnp.searchsorted(jnp.cumsum(tallies), jnp.arange(rows * top), side="right").astype(jnp.int32)
    listing = items.reshape(top, rows).T
    listing = listing[jax.random.permutation(jax.random.fold_in(own, 1), rows)]
    rotation = jax.random.randint(jax.random.fold_in(own, 2), (rows, 1), 0, top)
    return jnp.take_along_axis(listing, (jnp.arange(top)[None, :] + rotation) % top, axis=1)


def load_shares(number_of, total, reach, slope, full):
    loads = [(1 << 20) // math.isqrt(rank ** slope) + 1 for rank in range(1, number_of + 1)]
    largest = reach if full else min(reach, max(-(-total // number_of), total * loads[0] // sum(loads)))
    least = 1 if total - largest >= number_of - 1 else 0
    given, spare = [largest] + [least] * (number_of - 1), total - largest - least * (number_of - 1)
    while spare > 0:
        free = [i for i in range(1, number_of) if given[i] < largest] or [i for i in range(1, number_of) if given[i] < reach]
        mass, remaining = sum([loads[i] for i in free]), spare
        for i in free:
            addition = min(reach - given[i], max(1, remaining * loads[i] // mass), spare)
            given[i] = given[i] + addition
            spare = spare - addition
    return np.array(given)


def gaussian(key, shape, spread, bound, pieces=(), kind=jnp.bfloat16):
    values = jax.random.normal(key, shape, jnp.float32) * spread
    if len(pieces) > 0:
        values = block_scale(key, shape, pieces, -0.22, 0.18) * values
    return jnp.clip(values, min=-bound, max=bound).astype(kind)


def setup_inputs(seed: int = 0) -> dict:
    keys = jax.random.split(jax.random.key(seed), 8)
    tokens = gaussian(keys[0], (TOKENS, D), 1.0, 6.0, ((0, 256),))
    cotangent = gaussian(keys[1], (TOKENS, D), 1.0, 6.0, ((0, 256),))
    expert_ids_keys = jax.random.split(jax.random.fold_in(keys[2], 1), TOKENS // TOK_DEV)
    expert_ids_turns = jax.random.permutation(jax.random.fold_in(keys[2], 3), TOKENS // TOK_DEV)
    expert_ids = jax.vmap(lambda own, number: shared_out(jax.random.fold_in(keys[2], 2), own, number, TOK_DEV, EXPERTS, TOP, CAP, 2))(expert_ids_keys, expert_ids_turns).reshape((TOKENS, TOP))
    gate_values = jnp.clip(jnp.exp(math.log(0.5) - 2.306499 * jax.random.uniform(keys[3], (TOKENS, TOP), jnp.float32) ** block_scale(keys[3], (TOKENS, TOP), ((0, 256),), -0.2, 0.2)), 0.049804688, 0.5).astype(jnp.bfloat16)
    gate_weight = gaussian(keys[4], (EXPERTS * SPLIT, HID, D), D ** -0.5, 0.09375, ((0, 256),))
    up_weight = gaussian(keys[5], (EXPERTS * SPLIT, HID, D), D ** -0.5, 0.09375, ((0, 256),))
    down_weight = gaussian(keys[6], (EXPERTS * SPLIT, HID, D), FF ** -0.5, 0.15625, ((0, 256),))
    return dict(tokens=tokens, cotangent=cotangent, expert_ids=expert_ids, gate_values=gate_values, gate_weight=gate_weight, up_weight=up_weight, down_weight=down_weight)


def reference(tokens, cotangent, expert_ids, gate_values, gate_weight, up_weight, down_weight):
    route_count = TOKENS * TOP
    flat_ids = expert_ids.reshape(route_count).astype(jnp.int32)
    order_rows = jnp.argsort(flat_ids, stable=True).astype(jnp.int32)
    sorted_ids = flat_ids[order_rows]
    counts = jnp.sum((flat_ids[:, None] == jnp.arange(EXPERTS, dtype=jnp.int32)[None, :]).astype(jnp.int32), axis=0)
    starts = (jnp.cumsum(counts) - counts).astype(jnp.int32)
    rank_rows = jnp.arange(route_count, dtype=jnp.int32) - starts[sorted_ids]
    row_limit = N_EXPERT * N_TENSOR * CAP
    slot_table = jnp.full((EXPERTS, row_limit), route_count, jnp.int32).at[sorted_ids, rank_rows].set(order_rows)
    token_pad = jnp.concatenate([tokens, jnp.zeros((1, D), jnp.bfloat16)], axis=0)
    cot_pad = jnp.concatenate([cotangent, jnp.zeros((1, D), jnp.bfloat16)], axis=0)
    gate_pad = jnp.concatenate([gate_values.reshape(route_count), jnp.zeros((1,), jnp.bfloat16)], axis=0)
    gate_all = gate_weight.reshape(EXPERTS, SPLIT, HID, D)
    up_all = up_weight.reshape(EXPERTS, SPLIT, HID, D)
    down_all = down_weight.reshape(EXPERTS, SPLIT, HID, D)

    def one_expert(carry, expert_index):
        token_sum, gate_store = carry
        picked = slot_table[expert_index]
        owner_token = jnp.minimum(picked // TOP, TOKENS).astype(jnp.int32)
        inputs = token_pad[owner_token]
        cot_rows = cot_pad[owner_token]
        gate_rows = gate_pad[picked]
        gate_groups = gate_all[expert_index]
        up_groups = up_all[expert_index]
        down_groups = down_all[expert_index]
        w_gate = gate_groups.reshape(FF, D)
        w_up = up_groups.reshape(FF, D)
        w_down = down_groups.reshape(FF, D)
        pre_gate = jnp.dot(inputs, w_gate.T, preferred_element_type=jnp.float32)
        pre_up = jnp.dot(inputs, w_up.T, preferred_element_type=jnp.float32)
        sigmoid_gate = jax.nn.sigmoid(pre_gate)
        swish_gate = pre_gate * sigmoid_gate
        hidden = (swish_gate * pre_up).astype(jnp.bfloat16)
        hidden_groups = hidden.astype(jnp.float32).reshape(row_limit, SPLIT, HID)
        cot_wide = cot_rows.astype(jnp.float32)
        cot_proj = jnp.einsum("ld,gfd->lgf", cot_wide, down_groups.astype(jnp.float32))
        gate_part = jnp.sum(hidden_groups * cot_proj, axis=2).astype(jnp.bfloat16)
        gate_total = jnp.sum(gate_part.astype(jnp.float32), axis=1)
        scaled = (gate_rows.astype(jnp.float32)[:, None] * cot_wide).astype(jnp.bfloat16)
        d_hidden = jnp.dot(scaled, w_down.T, preferred_element_type=jnp.float32)
        d_pre_gate = (d_hidden * pre_up * sigmoid_gate * (1.0 + pre_gate * (1.0 - sigmoid_gate))).astype(jnp.bfloat16)
        d_pre_up = (d_hidden * swish_gate).astype(jnp.bfloat16)
        row_part = jnp.einsum("lgf,gfd->lgd", d_pre_gate.astype(jnp.float32).reshape(row_limit, SPLIT, HID), gate_groups.astype(jnp.float32))
        row_part = row_part + jnp.einsum("lgf,gfd->lgd", d_pre_up.astype(jnp.float32).reshape(row_limit, SPLIT, HID), up_groups.astype(jnp.float32))
        row_part = row_part.astype(jnp.bfloat16).astype(jnp.float32)
        d_row = jnp.sum(row_part, axis=1).astype(jnp.bfloat16).astype(jnp.float32)
        token_sum = token_sum.at[owner_token].add(d_row)
        gate_store = gate_store.at[picked].set(gate_total.astype(jnp.bfloat16).astype(jnp.float32))
        return (token_sum, gate_store), None

    start_carry = (jnp.zeros((TOKENS + 1, D), jnp.float32), jnp.zeros((route_count + 1,), jnp.float32))
    final_carry, unused = lax.scan(one_expert, start_carry, jnp.arange(EXPERTS, dtype=jnp.int32))
    token_sum, gate_store = final_carry
    d_tokens = token_sum[:TOKENS].astype(jnp.bfloat16)
    gate_grad = gate_store[:route_count].reshape(TOKENS, TOP).astype(jnp.bfloat16)
    return (d_tokens, gate_grad)
```

```python
import functools

import jax
import jax.numpy as jnp
from jax import lax
from jax.experimental import pallas as pl
from jax.experimental.pallas import tpu as pltpu
from jax.sharding import PartitionSpec as P

MESH = pl.DeviceIdType.MESH
BF = jnp.bfloat16
F32 = jnp.float32

D = 4096
HID = 384
TOK = 128
CAP = 3
NZ, NY, NC, NX = 8, 4, 2, 4
PEERS = NZ * NY * NC
SLOTS = PEERS * CAP
CHUNKS = 4
PER = PEERS // CHUNKS
ROWS = PER * CAP
MANY = ROWS * NX
LANES = 128
SUB = D // LANES
WIDE = D + LANES
HALF = D // 2
BACK = CAP * SUB + 16
ZORD = (0, 1, 6, 3, 5, 4, 7, 2)
NT = (((1,), (1,)), ((), ()))


def kernel(
    tok_hbm,
    cot_hbm,
    ids_ref,
    gate_ref,
    wg_hbm,
    wu_hbm,
    wd_hbm,
    dtok_hbm,
    ggrad_ref,
    src,
    wts,
    out_rows,
    in_rows,
    xrows,
    pre,
    part,
    relay,
    full,
    ret_out,
    ret_in,
    home,
    dtok,
    load_sem,
    w_sem,
    disp_send,
    disp_recv,
    ag_send,
    ag_recv,
    rs_send,
    rs_recv,
    ret_send,
    ret_recv,
    out_sem,
):
    expert = lax.axis_index("expert")
    tensor = lax.axis_index("tensor")
    mz, mc = expert // NC, expert % NC
    my, mx = tensor // NX, tensor % NX

    def device(z, c, y, x):
        return (z * NC + c, y * NX + x)

    def peer(sign, kz, j):
        ky, kc = j // NC, j % NC
        return device(
            lax.rem(mz + sign * kz + NZ, NZ),
            lax.rem(mc + kc, NC),
            lax.rem(my + sign * ky + NY, NY),
            mx,
        )

    right = device(mz, mc, my, lax.rem(mx + 1, NX))
    left = device(mz, mc, my, lax.rem(mx + NX - 1, NX))

    loads = [
        pltpu.make_async_copy(tok_hbm, src.at[0], load_sem.at[0]),
        pltpu.make_async_copy(cot_hbm, src.at[1], load_sem.at[1]),
    ]
    weight_loads = [
        pltpu.make_async_copy(w.at[0], wts.at[i], w_sem.at[i])
        for i, w in enumerate((wg_hbm, wu_hbm, wd_hbm))
    ]
    for copy in loads + weight_loads:
        copy.start()

    barrier = pltpu.get_barrier_semaphore()
    for q in range(NZ):

        def greet(j, carry, q=q):
            pl.semaphore_signal(
                barrier, inc=1, device_id=peer(1, ZORD[q], j), device_id_type=MESH
            )
            return carry

        lax.fori_loop(1 if q == 0 else 0, NY * NC, greet, 0)
    for neighbour in (left, right):
        pl.semaphore_signal(barrier, inc=1, device_id=neighbour, device_id_type=MESH)

    ids = ids_ref[...]
    t0 = lax.broadcasted_iota(jnp.int32, (TOK, TOK), 0)
    t1 = lax.broadcasted_iota(jnp.int32, (TOK, TOK), 1)
    ids_row = jnp.sum(jnp.where(t0 == t1, ids, 0), axis=0, keepdims=True)
    earlier = jnp.where((ids == ids_row) & (t1 < t0), 1, 0)
    position = jnp.sum(earlier, axis=1, keepdims=True)
    kz = ((ids >> 3) - mz) & (NZ - 1)
    kc = ((ids >> 2) - mc) & (NC - 1)
    ky = (ids - my) & (NY - 1)
    q_of = jnp.zeros_like(kz)
    for q in range(NZ):
        q_of = jnp.where(kz == ZORD[q], q, q_of)
    peer_of = (q_of * NY + ky) * NC + kc
    slot = peer_of * CAP + position
    slot_row = jnp.sum(jnp.where(t0 == t1, slot, 0), axis=0, keepdims=True)
    gate = gate_ref[...].astype(F32)

    def sort(c, h):
        at = lax.broadcasted_iota(jnp.int32, (ROWS, TOK), 0) + c * ROWS
        pick = jnp.where(at == slot_row, 1.0, 0.0).astype(BF)
        for j in range(0, D, 2048):
            rows = jnp.dot(pick, src[h, :, j : j + 2048], preferred_element_type=F32)
            out_rows[h, pl.ds(c * ROWS, ROWS), j // LANES : (j + 2048) // LANES, :] = (
                pltpu.einshape("a(bc)->abc", rows.astype(BF), c=LANES)
            )

    def dispatch(c, h):
        for q in range(c * NZ // CHUNKS, (c + 1) * NZ // CHUNKS):

            def send(j, carry, q=q):
                at = pl.ds((q * NY * NC + j) * CAP, CAP)
                pltpu.make_async_remote_copy(
                    src_ref=out_rows.at[h, at],
                    dst_ref=in_rows.at[h, at],
                    send_sem=disp_send.at[h, c],
                    recv_sem=disp_recv.at[h, c],
                    device_id=peer(1, ZORD[q], j),
                    device_id_type=MESH,
                ).start()
                return carry

            lax.fori_loop(1 if q == 0 else 0, NY * NC, send, 0)

    def remote_slots(c):
        skip = CAP if c == 0 else 0
        return pl.ds(c * ROWS + skip, ROWS - skip)

    def gather_copy(c, h, kind):
        x = xrows.at[h, c]
        own, from_left, far, from_right = (pl.ds(i * ROWS, ROWS) for i in range(4))
        a, b = pl.ds(0, HALF), pl.ds(HALF, HALF)
        ref_pair, to = (
            ((x.at[own], x.at[from_left]), right),
            ((x.at[own], x.at[from_right]), left),
            ((x.at[from_left, a], x.at[far, a]), right),
            ((x.at[from_right, b], x.at[far, b]), left),
        )[kind]
        return pltpu.make_async_remote_copy(
            src_ref=ref_pair[0],
            dst_ref=ref_pair[1],
            send_sem=ag_send.at[h, c, kind],
            recv_sem=ag_recv.at[h, c, kind],
            device_id=to,
            device_id_type=MESH,
        )

    def arrive(c, h):
        at = remote_slots(c)
        pltpu.make_async_copy(
            out_rows.at[h, at], in_rows.at[h, at], disp_recv.at[h, c]
        ).wait()
        if c == 0:
            in_rows[h, 0:CAP] = out_rows[h, 0:CAP]
        for j in range(0, SUB, 16):
            xrows[h, c, 0:ROWS, j * LANES : (j + 16) * LANES] = pltpu.einshape(
                "abc->a(bc)", in_rows[h, pl.ds(c * ROWS, ROWS), j : j + 16, :]
            )
        gather_copy(c, h, 0).start()
        gather_copy(c, h, 1).start()

    def forward(c, h):
        gather_copy(c, h, 0).wait_recv()
        gather_copy(c, h, 2).start()
        gather_copy(c, h, 1).wait_recv()
        gather_copy(c, h, 3).start()

    def compute(c, h):
        gather_copy(c, h, 2).wait_recv()
        gather_copy(c, h, 3).wait_recv()
        if h == 0:
            if c == 0:
                weight_loads[0].wait()
                weight_loads[1].wait()
            pre[0] = lax.dot_general(
                xrows[0, c], wts[0], NT, preferred_element_type=F32
            )
            pre[1] = lax.dot_general(
                xrows[0, c], wts[1], NT, preferred_element_type=F32
            )
            return
        if c == 0:
            weight_loads[2].wait()
        d_hidden = lax.dot_general(
            xrows[1, c], wts[2], NT, preferred_element_type=F32
        )
        pre_gate, pre_up = pre[0], pre[1]
        sigmoid_gate = jax.nn.sigmoid(pre_gate)
        swish_gate = pre_gate * sigmoid_gate
        hidden = (swish_gate * pre_up).astype(BF).astype(F32)
        gate_part = jnp.sum(hidden * d_hidden, axis=1, keepdims=True)
        part[c, :, D:WIDE] = jnp.broadcast_to(gate_part, (MANY, LANES)).astype(BF)
        d_gate = (
            d_hidden * pre_up * sigmoid_gate * (1.0 + pre_gate * (1.0 - sigmoid_gate))
        ).astype(BF)
        d_up = (d_hidden * swish_gate).astype(BF)
        for j in range(0, D, 512):
            if j == HALF:
                scatter_copy(c, 0).start()
                scatter_copy(c, 3).start()
            at = slice(j, j + 512)
            part[c, :, at] = (
                jnp.dot(d_gate, wts[0, :, at], preferred_element_type=F32)
                + jnp.dot(d_up, wts[1, :, at], preferred_element_type=F32)
            ).astype(BF)
        scatter_copy(c, 1).start()
        scatter_copy(c, 2).start()

    def scatter_copy(c, kind):
        p = part.at[c]
        from_left_rows, far, from_right_rows = (pl.ds(i * ROWS, ROWS) for i in (1, 2, 3))
        a, b = pl.ds(0, HALF), pl.ds(HALF, WIDE - HALF)
        ref_pair, to = (
            ((p.at[far, a], relay.at[c, :, a]), right),
            ((p.at[far, b], relay.at[c, :, b]), left),
            ((p.at[from_right_rows, b], full.at[c, 0, :, b]), right),
            ((p.at[from_left_rows, a], full.at[c, 1, :, a]), left),
            ((p.at[from_right_rows, a], full.at[c, 0, :, a]), right),
            ((p.at[from_left_rows, b], full.at[c, 1, :, b]), left),
        )[kind]
        return pltpu.make_async_remote_copy(
            src_ref=ref_pair[0],
            dst_ref=ref_pair[1],
            send_sem=rs_send.at[c, kind],
            recv_sem=rs_recv.at[c, kind],
            device_id=to,
            device_id_type=MESH,
        )

    def pass_on(c):
        for kind, rows, cols in (
            (0, slice(3 * ROWS, 4 * ROWS), slice(0, HALF)),
            (1, slice(ROWS, 2 * ROWS), slice(HALF, WIDE)),
        ):
            scatter_copy(c, kind).wait_recv()
            part[c, rows, cols] = (
                part[c, rows, cols].astype(F32) + relay[c, :, cols].astype(F32)
            ).astype(BF)
            scatter_copy(c, kind + 4).start()

    def send_home(c):
        for kind in (2, 3, 4, 5):
            scatter_copy(c, kind).wait_recv()

        def total(at):
            return (
                part[c, 0:ROWS, at].astype(F32)
                + full[c, 0, :, at].astype(F32)
                + full[c, 1, :, at].astype(F32)
            ).astype(BF)

        for j in range(0, D, 2048):
            tiles = pltpu.einshape("a(bc)->abc", total(slice(j, j + 2048)), c=LANES)
            for i in range(PER):
                for p in range(CAP):
                    at = p * SUB + j // LANES
                    ret_out[c * PER + i, at : at + 16, :] = tiles[i * CAP + p]
        r0 = lax.broadcasted_iota(jnp.int32, (PER * 16, ROWS), 0)
        r1 = lax.broadcasted_iota(jnp.int32, (PER * 16, ROWS), 1)
        spread = jnp.where(
            (r1 == (r0 >> 4) * CAP + (r0 & 15)) & ((r0 & 15) < CAP), 1.0, 0.0
        ).astype(BF)
        gates = jnp.dot(spread, total(slice(D, WIDE)), preferred_element_type=F32)
        ret_out[c * PER : (c + 1) * PER, CAP * SUB : BACK, :] = gates.astype(BF).reshape(
            PER, 16, LANES
        )
        for q in range(c * NZ // CHUNKS, (c + 1) * NZ // CHUNKS):

            def send(j, carry, q=q):
                at = q * NY * NC + j
                pltpu.make_async_remote_copy(
                    src_ref=ret_out.at[at],
                    dst_ref=ret_in.at[at],
                    send_sem=ret_send.at[c],
                    recv_sem=ret_recv.at[c],
                    device_id=peer(-1, ZORD[q], j),
                    device_id_type=MESH,
                ).start()
                return carry

            lax.fori_loop(1 if q == 0 else 0, NY * NC, send, 0)
        if c == 0:
            ret_in[0] = ret_out[0]

    def returned(c):
        skip = 1 if c == 0 else 0
        return pl.ds(c * PER + skip, PER - skip)

    def come_home(c):
        at = returned(c)
        pltpu.make_async_copy(ret_out.at[at], ret_in.at[at], ret_recv.at[c]).wait()
        rows = ret_in[c * PER : (c + 1) * PER, 0 : CAP * SUB, :].reshape(
            ROWS, SUB, LANES
        )
        for j in range(0, SUB, 16):
            home[c * ROWS : (c + 1) * ROWS, j * LANES : (j + 16) * LANES] = (
                pltpu.einshape("abc->a(bc)", rows[:, j : j + 16, :])
            )

    def finish():
        at = lax.broadcasted_iota(jnp.int32, (TOK, SLOTS), 1)
        pick = jnp.where(at == slot, 1.0, 0.0).astype(BF)
        for j in range(0, D, 1024):
            dtok[:, j : j + 1024] = jnp.dot(
                pick, home[:, j : j + 1024], preferred_element_type=F32
            ).astype(BF)
        out = pltpu.make_async_copy(dtok, dtok_hbm, out_sem)
        out.start()
        at = lax.broadcasted_iota(jnp.int32, (TOK, PEERS * 16), 1)
        pick = jnp.where(at == peer_of * 16 + position, 1.0, 0.0).astype(BF)
        gates = jnp.dot(
            pick,
            ret_in[:, CAP * SUB : BACK, :].reshape(PEERS * 16, LANES),
            preferred_element_type=F32,
        )
        ggrad_ref[...] = (gates[:, 0:1] / gate).astype(BF)
        out.wait()

    def drain():
        for c in range(CHUNKS):
            for h in range(2):
                at = remote_slots(c)
                pltpu.make_async_copy(
                    out_rows.at[h, at], in_rows.at[h, at], disp_send.at[h, c]
                ).wait()
                for kind in range(4):
                    gather_copy(c, h, kind).wait_send()
            for kind in range(6):
                scatter_copy(c, kind).wait_send()
            at = returned(c)
            pltpu.make_async_copy(ret_out.at[at], ret_in.at[at], ret_send.at[c]).wait()

    loads[0].wait()
    sort(0, 0)
    pl.semaphore_wait(barrier, PEERS - 1 + 2)
    dispatch(0, 0)
    loads[1].wait()
    for j in range(0, D, 1024):
        src[1, :, j : j + 1024] = (gate * src[1, :, j : j + 1024].astype(F32)).astype(BF)

    def sd(c, h):
        sort(c, h)
        dispatch(c, h)

    sd(0, 1)
    sd(1, 0)
    sd(1, 1)
    arrive(0, 0)
    arrive(0, 1)
    sd(2, 0)
    sd(2, 1)
    forward(0, 0)
    sd(3, 0)
    sd(3, 1)
    arrive(1, 0)
    forward(0, 1)
    compute(0, 0)
    arrive(1, 1)
    forward(1, 0)
    compute(0, 1)
    arrive(2, 0)
    forward(1, 1)
    compute(1, 0)
    pass_on(0)
    arrive(2, 1)
    forward(2, 0)
    compute(1, 1)
    send_home(0)
    arrive(3, 0)
    forward(2, 1)
    compute(2, 0)
    pass_on(1)
    arrive(3, 1)
    forward(3, 0)
    compute(2, 1)
    send_home(1)
    forward(3, 1)
    compute(3, 0)
    pass_on(2)
    compute(3, 1)
    send_home(2)
    come_home(0)
    come_home(1)
    pass_on(3)
    come_home(2)
    send_home(3)
    come_home(3)
    finish()
    drain()


def local(tokens, cotangent, expert_ids, gate_values, gate_weight, up_weight, down_weight):
    vmem = pl.BlockSpec(memory_space=pltpu.VMEM)
    hbm = pl.BlockSpec(memory_space=pl.ANY)
    dma = pltpu.SemaphoreType.DMA
    return pl.pallas_call(
        kernel,
        out_shape=(
            jax.ShapeDtypeStruct((TOK, D), BF),
            jax.ShapeDtypeStruct((TOK, 1), BF),
        ),
        in_specs=[hbm, hbm, vmem, vmem, hbm, hbm, hbm],
        out_specs=(hbm, vmem),
        scratch_shapes=[
            pltpu.VMEM((2, TOK, D), BF),
            pltpu.VMEM((3, HID, D), BF),
            pltpu.VMEM((2, SLOTS, SUB, LANES), BF),
            pltpu.VMEM((2, SLOTS, SUB, LANES), BF),
            pltpu.VMEM((2, CHUNKS, MANY, D), BF),
            pltpu.VMEM((2, MANY, HID), F32),
            pltpu.VMEM((CHUNKS, MANY, WIDE), BF),
            pltpu.VMEM((CHUNKS, ROWS, WIDE), BF),
            pltpu.VMEM((CHUNKS, 2, ROWS, WIDE), BF),
            pltpu.VMEM((PEERS, BACK, LANES), BF),
            pltpu.VMEM((PEERS, BACK, LANES), BF),
            pltpu.VMEM((SLOTS, D), BF),
            pltpu.VMEM((TOK, D), BF),
            dma((2,)),
            dma((3,)),
            dma((2, CHUNKS)),
            dma((2, CHUNKS)),
            dma((2, CHUNKS, 4)),
            dma((2, CHUNKS, 4)),
            dma((CHUNKS, 6)),
            dma((CHUNKS, 6)),
            dma((CHUNKS,)),
            dma((CHUNKS,)),
            dma,
        ],
        compiler_params=pltpu.CompilerParams(
            collective_id=0, has_side_effects=True, vmem_limit_bytes=60 * 2**20
        ),
    )(tokens, cotangent, expert_ids, gate_values, gate_weight, up_weight, down_weight)


def solution(mesh):
    rows = P(("expert", "tensor"), None)
    blocks = P(("expert", "tensor"), None, None)
    return jax.shard_map(
        local,
        mesh=mesh,
        in_specs=(rows, rows, rows, rows, blocks, blocks, blocks),
        out_specs=(rows, rows),
        check_vma=False,
    )
```

```python
import functools

import jax
import jax.numpy as jnp
from jax import lax
from jax.experimental import pallas as pl
from jax.experimental.pallas import tpu as pltpu
from jax.sharding import PartitionSpec as P

MESH = pl.DeviceIdType.MESH
BF = jnp.bfloat16
F32 = jnp.float32

D = 4096
HID = 384
TOK = 128
CAP = 3
NZ, NY, NC, NX = 8, 4, 2, 4
PEERS = NZ * NY * NC
SLOTS = PEERS * CAP
CHUNKS = 4
PER = PEERS // CHUNKS
ROWS = PER * CAP
MANY = ROWS * NX
LANES = 128
SUB = D // LANES
WIDE = D + LANES
HALF = D // 2
KTILE = 1024
NTILE = 512
STEP = 2048
UNSORT = 2048
PIECE = CAP * SUB // 2
BACK = CAP * SUB + 16
ZORD = (0, 1, 4, 7, 3, 5, 2, 6)
NT = (((1,), (1,)), ((), ()))


def kernel(
    tok_hbm,
    cot_hbm,
    ids_ref,
    gate_ref,
    wg_hbm,
    wu_hbm,
    wd_hbm,
    home_hbm,
    ggrad_ref,
    slot_ref,
    src,
    wts,
    out_rows,
    in_rows,
    xrows,
    pre,
    grads,
    part,
    relay,
    full,
    ret_out,
    ret_in,
    home,
    load_sem,
    w_sem,
    disp_send,
    disp_recv,
    ag_send,
    ag_recv,
    rs_send,
    rs_recv,
    ret_send,
    ret_recv,
    out_sem,
):
    expert = lax.axis_index("expert")
    tensor = lax.axis_index("tensor")
    mz, mc = expert // NC, expert % NC
    my, mx = tensor // NX, tensor % NX

    def device(z, c, y, x):
        return (z * NC + c, y * NX + x)

    def each_peer(first, last, sign, act):
        def plane(q, carry):
            kz = jnp.int32(ZORD[0])
            for i in range(1, NZ):
                kz = jnp.where(q == i, ZORD[i], kz)
            z = lax.rem(mz + sign * kz + NZ, NZ)
            for j in range(NY * NC):
                y = lax.rem(my + sign * (j // NC) + NY, NY)
                to = device(z, lax.rem(mc + j % NC, NC), y, mx)
                k = q * NY * NC + j
                if j == 0:
                    pl.when(q > 0)(functools.partial(act, k, to))
                else:
                    act(k, to)
            return carry

        lax.fori_loop(first, last, plane, 0)

    right = device(mz, mc, my, lax.rem(mx + 1, NX))
    left = device(mz, mc, my, lax.rem(mx + NX - 1, NX))

    loads = [
        pltpu.make_async_copy(tok_hbm, src.at[0], load_sem.at[0]),
        pltpu.make_async_copy(cot_hbm, src.at[1], load_sem.at[1]),
    ]
    weight_loads = [
        pltpu.make_async_copy(w.at[0], wts.at[i], w_sem.at[i])
        for i, w in enumerate((wg_hbm, wu_hbm, wd_hbm))
    ]
    for copy in loads + weight_loads:
        copy.start()

    barrier = pltpu.get_barrier_semaphore()

    def greet(k, to):
        pl.semaphore_signal(barrier, inc=1, device_id=to, device_id_type=MESH)

    each_peer(0, NZ, 1, greet)
    for neighbour in (left, right):
        pl.semaphore_signal(barrier, inc=1, device_id=neighbour, device_id_type=MESH)

    t0 = lax.broadcasted_iota(jnp.int32, (TOK, TOK), 0)
    t1 = lax.broadcasted_iota(jnp.int32, (TOK, TOK), 1)
    ids_row = ids_ref[...]
    ids = jnp.sum(jnp.where(t0 == t1, ids_row, 0), axis=1, keepdims=True)
    earlier = jnp.where((ids == ids_row) & (t1 < t0), 1, 0)
    position = jnp.sum(earlier, axis=1, keepdims=True)
    kz = ((ids >> 3) - mz) & (NZ - 1)
    kc = ((ids >> 2) - mc) & (NC - 1)
    ky = (ids - my) & (NY - 1)
    q_of = jnp.zeros_like(kz)
    for q in range(NZ):
        q_of = jnp.where(kz == ZORD[q], q, q_of)
    peer_of = (q_of * NY + ky) * NC + kc
    slot = peer_of * CAP + position
    slot_row = jnp.sum(jnp.where(t0 == t1, slot, 0), axis=0, keepdims=True)
    gate = jnp.sum(
        jnp.where(t0 == t1, gate_ref[...].astype(F32), 0.0), axis=1, keepdims=True
    )

    def columns(j):
        return pl.ds(pl.multiple_of(j * STEP, STEP), STEP)

    def tiles(j):
        return pl.ds(pl.multiple_of(j * (STEP // LANES), STEP // LANES), STEP // LANES)

    def sort(c, h):
        at = lax.broadcasted_iota(jnp.int32, (ROWS, TOK), 0) + c * ROWS
        pick = jnp.where(at == slot_row, 1.0, 0.0).astype(BF)

        def tile(j, carry):
            rows = jnp.dot(pick, src[h, :, columns(j)], preferred_element_type=F32)
            out_rows[h, pl.ds(c * ROWS, ROWS), tiles(j), :] = pltpu.einshape(
                "a(bc)->abc", rows.astype(BF), c=LANES
            )
            return carry

        lax.fori_loop(0, D // STEP, tile, 0)

    def dispatch(c, h):

        def send(k, to):
            at = pl.ds(k * CAP, CAP)
            pltpu.make_async_remote_copy(
                src_ref=out_rows.at[h, at],
                dst_ref=in_rows.at[h, at],
                send_sem=disp_send.at[h, c],
                recv_sem=disp_recv.at[h, c],
                device_id=to,
                device_id_type=MESH,
            ).start()

        each_peer(c * NZ // CHUNKS, (c + 1) * NZ // CHUNKS, 1, send)

    def await_dispatch(c, h, sem):
        def wait(at):
            pltpu.make_async_copy(
                out_rows.at[h, at], in_rows.at[h, at], sem.at[h, c]
            ).wait()

        @pl.when(c == 0)
        def _():
            wait(pl.ds(CAP, ROWS - CAP))

        @pl.when(c > 0)
        def _():
            wait(pl.ds(c * ROWS, ROWS))

    def gather_copy(c, h, kind):
        x = xrows.at[h, c]
        own, from_left, far, from_right = (pl.ds(i * ROWS, ROWS) for i in range(4))
        a, b = pl.ds(0, HALF), pl.ds(HALF, HALF)
        ref_pair, to = (
            ((x.at[own], x.at[from_left]), right),
            ((x.at[own], x.at[from_right]), left),
            ((x.at[from_left, a], x.at[far, a]), right),
            ((x.at[from_right, b], x.at[far, b]), left),
        )[kind]
        return pltpu.make_async_remote_copy(
            src_ref=ref_pair[0],
            dst_ref=ref_pair[1],
            send_sem=ag_send.at[h, c, kind],
            recv_sem=ag_recv.at[h, c, kind],
            device_id=to,
            device_id_type=MESH,
        )

    def arrive(c, h):
        await_dispatch(c, h, disp_recv)

        @pl.when(c == 0)
        def _():
            in_rows[h, 0:CAP] = out_rows[h, 0:CAP]

        def tile(j, carry):
            xrows[h, c, 0:ROWS, columns(j)] = pltpu.einshape(
                "abc->a(bc)", in_rows[h, pl.ds(c * ROWS, ROWS), tiles(j), :]
            )
            return carry

        lax.fori_loop(0, D // STEP, tile, 0)
        gather_copy(c, h, 0).start()
        gather_copy(c, h, 1).start()

    def forward(c, h):
        gather_copy(c, h, 0).wait_recv()
        gather_copy(c, h, 2).start()
        gather_copy(c, h, 1).wait_recv()
        gather_copy(c, h, 3).start()

    def project(c, h, w):
        pre[w] = jnp.zeros((MANY, HID), F32)

        def add(k, carry):
            at = pl.ds(pl.multiple_of(k * KTILE, KTILE), KTILE)
            pre[w] += lax.dot_general(
                xrows[h, c, :, at], wts[w, :, at], NT, preferred_element_type=F32
            )
            return carry

        lax.fori_loop(0, D // KTILE, add, 0)

    def compute(c, h):
        gather_copy(c, h, 2).wait_recv()
        gather_copy(c, h, 3).wait_recv()
        if h == 0:

            @pl.when(c == 0)
            def _():
                weight_loads[0].wait()
                weight_loads[1].wait()

            project(c, 0, 0)
            project(c, 0, 1)
            return

        @pl.when(c == 0)
        def _():
            weight_loads[2].wait()

        project(c, 1, 2)
        pre_gate, pre_up, d_hidden = pre[0], pre[1], pre[2]
        sigmoid_gate = jax.nn.sigmoid(pre_gate)
        swish_gate = pre_gate * sigmoid_gate
        hidden = (swish_gate * pre_up).astype(BF).astype(F32)
        gate_part = jnp.sum(hidden * d_hidden, axis=1, keepdims=True)
        part[c, :, D:WIDE] = jnp.broadcast_to(gate_part, (MANY, LANES)).astype(BF)
        d_gate = (
            d_hidden * pre_up * sigmoid_gate * (1.0 + pre_gate * (1.0 - sigmoid_gate))
        ).astype(BF)
        d_up = (d_hidden * swish_gate).astype(BF)
        grads[0] = d_gate
        grads[1] = d_up

        def unproject(k, carry):
            at = pl.ds(pl.multiple_of(k * NTILE, NTILE), NTILE)
            part[c, :, at] = (
                jnp.dot(grads[0], wts[0, :, at], preferred_element_type=F32)
                + jnp.dot(grads[1], wts[1, :, at], preferred_element_type=F32)
            ).astype(BF)
            return carry

        for t in range(2):
            lax.fori_loop(
                t * HALF // NTILE, (t + 1) * HALF // NTILE, unproject, 0
            )
            for kind in range(4):
                scatter_copy(c, t, kind).start()

    def scatter_columns(t, side):
        start = t * HALF + side * HALF // 2
        return start, (WIDE if t == 1 and side == 1 else start + HALF // 2)

    def scatter_copy(c, t, kind):
        p = part.at[c]
        from_left_rows, far, from_right_rows = (pl.ds(i * ROWS, ROWS) for i in (1, 2, 3))
        a, b = (pl.ds(i, j - i) for i, j in (scatter_columns(t, 0), scatter_columns(t, 1)))
        ref_pair, to = (
            ((p.at[far, a], relay.at[c, :, a]), right),
            ((p.at[far, b], relay.at[c, :, b]), left),
            ((p.at[from_right_rows, b], full.at[c, 0, :, b]), right),
            ((p.at[from_left_rows, a], full.at[c, 1, :, a]), left),
            ((p.at[from_right_rows, a], full.at[c, 0, :, a]), right),
            ((p.at[from_left_rows, b], full.at[c, 1, :, b]), left),
        )[kind]
        return pltpu.make_async_remote_copy(
            src_ref=ref_pair[0],
            dst_ref=ref_pair[1],
            send_sem=rs_send.at[c, t, kind],
            recv_sem=rs_recv.at[c, t, kind],
            device_id=to,
            device_id_type=MESH,
        )

    def pass_on(c, t):
        for kind, rows in ((0, slice(3 * ROWS, 4 * ROWS)), (1, slice(ROWS, 2 * ROWS))):
            scatter_copy(c, t, kind).wait_recv()
            cols = slice(*scatter_columns(t, kind))
            part[c, rows, cols] = (
                part[c, rows, cols].astype(F32) + relay[c, :, cols].astype(F32)
            ).astype(BF)
            scatter_copy(c, t, kind + 4).start()

    def send_home(c, t):
        for kind in (2, 3, 4, 5):
            scatter_copy(c, t, kind).wait_recv()

        def total(at):
            return (
                part[c, 0:ROWS, at].astype(F32)
                + full[c, 0, :, at].astype(F32)
                + full[c, 1, :, at].astype(F32)
            ).astype(BF)

        rows = pltpu.einshape(
            "a(bc)->abc", total(slice(t * HALF, (t + 1) * HALF)), c=LANES
        )
        ret_out[pl.ds(c * PER, PER), t * PIECE : (t + 1) * PIECE, :] = rows.reshape(
            PER, PIECE, LANES
        )
        if t == 1:
            r0 = lax.broadcasted_iota(jnp.int32, (PER * 16, ROWS), 0)
            r1 = lax.broadcasted_iota(jnp.int32, (PER * 16, ROWS), 1)
            spread = jnp.where(
                (r1 == (r0 >> 4) * CAP + (r0 & 15)) & ((r0 & 15) < CAP), 1.0, 0.0
            ).astype(BF)
            gates = jnp.dot(spread, total(slice(D, WIDE)), preferred_element_type=F32)
            ret_out[pl.ds(c * PER, PER), CAP * SUB : BACK, :] = gates.astype(BF).reshape(
                PER, 16, LANES
            )

        def send(k, to):
            pltpu.make_async_remote_copy(
                src_ref=ret_out.at[k, returned(t)],
                dst_ref=ret_in.at[k, returned(t)],
                send_sem=ret_send.at[c, t],
                recv_sem=ret_recv.at[c, t],
                device_id=to,
                device_id_type=MESH,
            ).start()

        each_peer(c * NZ // CHUNKS, (c + 1) * NZ // CHUNKS, -1, send)

        @pl.when(c == 0)
        def _():
            ret_in[0, returned(t)] = ret_out[0, returned(t)]

    def returned(t):
        return pl.ds(0, PIECE) if t == 0 else pl.ds(PIECE, BACK - PIECE)

    def await_return(c, t, sem):
        def wait(at):
            pltpu.make_async_copy(
                ret_out.at[at, returned(t)], ret_in.at[at, returned(t)], sem.at[c, t]
            ).wait()

        @pl.when(c == 0)
        def _():
            wait(pl.ds(1, PER - 1))

        @pl.when(c > 0)
        def _():
            wait(pl.ds(c * PER, PER))

    def home_copy(c):
        at = pl.ds(c * ROWS, ROWS)
        return pltpu.make_async_copy(home.at[at], home_hbm.at[at], out_sem.at[c])

    def come_home(c):
        for t in range(2):
            await_return(c, t, ret_recv)
            rows = ret_in[pl.ds(c * PER, PER), t * PIECE : (t + 1) * PIECE, :]
            home[pl.ds(c * ROWS, ROWS), t * HALF : (t + 1) * HALF] = pltpu.einshape(
                "abc->a(bc)", rows.reshape(ROWS, SUB // 2, LANES)
            )
        home_copy(c).start()

    def finish():
        at = lax.broadcasted_iota(jnp.int32, (TOK, PEERS * 16), 1)
        pick = jnp.where(at == peer_of * 16 + position, 1.0, 0.0).astype(BF)
        gates = jnp.dot(
            pick,
            ret_in[:, CAP * SUB : BACK, :].reshape(PEERS * 16, LANES),
            preferred_element_type=F32,
        )
        ggrad = jnp.where(t0 == t1, gates / gate, 0.0)
        ggrad_ref[...] = jnp.sum(ggrad, axis=0, keepdims=True)
        slot_ref[...] = slot_row

    def drain():
        def ended(c, carry):
            for h in range(2):
                await_dispatch(c, h, disp_send)
                for kind in range(4):
                    gather_copy(c, h, kind).wait_send()
            for t in range(2):
                for kind in range(6):
                    scatter_copy(c, t, kind).wait_send()
                await_return(c, t, ret_send)
            home_copy(c).wait()
            return carry

        lax.fori_loop(0, CHUNKS, ended, 0)

    loads[0].wait()
    sort(0, 0)
    pl.semaphore_wait(barrier, PEERS - 1 + 2)
    dispatch(0, 0)
    loads[1].wait()
    for j in range(0, D, 1024):
        src[1, :, j : j + 1024] = (gate * src[1, :, j : j + 1024].astype(F32)).astype(BF)

    def sd(c, h):
        sort(c, h)
        dispatch(c, h)

    sd(0, 1)
    arrive(0, 0)
    lax.fori_loop(2, 4, lambda n, carry: sd(n // 2, n % 2) or carry, 0)
    arrive(0, 1)
    lax.fori_loop(4, 6, lambda n, carry: sd(n // 2, n % 2) or carry, 0)
    forward(0, 0)
    lax.fori_loop(6, 8, lambda n, carry: sd(n // 2, n % 2) or carry, 0)

    def step(c, carry):
        @pl.when(c < CHUNKS - 1)
        def _():
            arrive(c + 1, 0)

        forward(c, 1)
        compute(c, 0)

        @pl.when(c > 0)
        def _():
            pass_on(c - 1, 0)
            pass_on(c - 1, 1)

        @pl.when(c < CHUNKS - 1)
        def _():
            arrive(c + 1, 1)
            forward(c + 1, 0)

        compute(c, 1)

        @pl.when(c > 0)
        def _():
            send_home(c - 1, 0)
            send_home(c - 1, 1)

        return carry

    lax.fori_loop(0, CHUNKS, step, 0)
    pass_on(CHUNKS - 1, 0)
    pass_on(CHUNKS - 1, 1)
    lax.fori_loop(0, 2, lambda c, carry: come_home(c) or carry, 0)
    send_home(CHUNKS - 1, 0)
    send_home(CHUNKS - 1, 1)
    lax.fori_loop(2, CHUNKS, lambda c, carry: come_home(c) or carry, 0)
    finish()
    drain()


def unsort(home_ref, gate_ref, slot_ref, dtok_ref, ggrad_ref):
    t0 = lax.broadcasted_iota(jnp.int32, (TOK, TOK), 0)
    t1 = lax.broadcasted_iota(jnp.int32, (TOK, TOK), 1)
    slot = jnp.sum(jnp.where(t0 == t1, slot_ref[...], 0), axis=1, keepdims=True)
    at = lax.broadcasted_iota(jnp.int32, (TOK, SLOTS), 1)
    pick = jnp.where(at == slot, 1.0, 0.0).astype(BF)
    dtok_ref[...] = jnp.dot(pick, home_ref[...], preferred_element_type=F32).astype(BF)
    ggrad_ref[...] = gate_ref[...].astype(BF)


def local(tokens, cotangent, expert_ids, gate_values, gate_weight, up_weight, down_weight):
    vmem = pl.BlockSpec(memory_space=pltpu.VMEM)
    hbm = pl.BlockSpec(memory_space=pl.ANY)
    dma = pltpu.SemaphoreType.DMA
    home, gate_grad, slot = pl.pallas_call(
        kernel,
        out_shape=(
            jax.ShapeDtypeStruct((SLOTS, D), BF),
            jax.ShapeDtypeStruct((1, TOK), F32),
            jax.ShapeDtypeStruct((1, TOK), jnp.int32),
        ),
        in_specs=[hbm, hbm, vmem, vmem, hbm, hbm, hbm],
        out_specs=(hbm, vmem, vmem),
        scratch_shapes=[
            pltpu.VMEM((2, TOK, D), BF),
            pltpu.VMEM((3, HID, D), BF),
            pltpu.VMEM((2, SLOTS, SUB, LANES), BF),
            pltpu.VMEM((2, SLOTS, SUB, LANES), BF),
            pltpu.VMEM((2, CHUNKS, MANY, D), BF),
            pltpu.VMEM((3, MANY, HID), F32),
            pltpu.VMEM((2, MANY, HID), BF),
            pltpu.VMEM((CHUNKS, MANY, WIDE), BF),
            pltpu.VMEM((CHUNKS, ROWS, WIDE), BF),
            pltpu.VMEM((CHUNKS, 2, ROWS, WIDE), BF),
            pltpu.VMEM((PEERS, BACK, LANES), BF),
            pltpu.VMEM((PEERS, BACK, LANES), BF),
            pltpu.VMEM((SLOTS, D), BF),
            dma((2,)),
            dma((3,)),
            dma((2, CHUNKS)),
            dma((2, CHUNKS)),
            dma((2, CHUNKS, 4)),
            dma((2, CHUNKS, 4)),
            dma((CHUNKS, 2, 6)),
            dma((CHUNKS, 2, 6)),
            dma((CHUNKS, 2)),
            dma((CHUNKS, 2)),
            dma((CHUNKS,)),
        ],
        compiler_params=pltpu.CompilerParams(
            collective_id=0, has_side_effects=True, vmem_limit_bytes=60 * 2**20
        ),
    )(
        tokens,
        cotangent,
        expert_ids.reshape(1, TOK),
        gate_values.reshape(1, TOK),
        gate_weight,
        up_weight,
        down_weight,
    )
    d_tokens, gate_grad = pl.pallas_call(
        unsort,
        grid=(D // UNSORT,),
        out_shape=(
            jax.ShapeDtypeStruct((TOK, D), BF),
            jax.ShapeDtypeStruct((1, TOK), BF),
        ),
        in_specs=[
            pl.BlockSpec((SLOTS, UNSORT), lambda j: (0, j)),
            pl.BlockSpec((1, TOK), lambda j: (0, 0)),
            pl.BlockSpec((1, TOK), lambda j: (0, 0)),
        ],
        out_specs=(
            pl.BlockSpec((TOK, UNSORT), lambda j: (0, j)),
            pl.BlockSpec((1, TOK), lambda j: (0, 0)),
        ),
    )(home, gate_grad, slot)
    return d_tokens, gate_grad.reshape(TOK, 1)


def solution(mesh):
    rows = P(("expert", "tensor"), None)
    blocks = P(("expert", "tensor"), None, None)
    return jax.shard_map(
        local,
        mesh=mesh,
        in_specs=(rows, rows, rows, rows, blocks, blocks, blocks),
        out_specs=(rows, rows),
        check_vma=False,
    )
```

```python
import functools

import jax
import jax.numpy as jnp
from jax import lax
from jax.experimental import pallas as pl
from jax.experimental.pallas import tpu as pltpu
from jax.sharding import PartitionSpec as P

MESH = pl.DeviceIdType.MESH
BF = jnp.bfloat16
F32 = jnp.float32

D = 4096
HID = 384
TOK = 128
CAP = 3
NZ, NY, NC, NX = 8, 4, 2, 4
PEERS = NZ * NY * NC
SLOTS = PEERS * CAP
CHUNKS = 4
PER = PEERS // CHUNKS
ROWS = PER * CAP
MANY = ROWS * NX
LANES = 128
SUB = D // LANES
WIDE = LANES + D
HALF = D // 2
KTILE = 1024
NTILE = 512
SPLIT = 2
PIECES = 2 * SPLIT
SPAN = D // SPLIT
PSUB = SPAN // LANES
STEP = 2048
UNSORT = 2048
PIECE = CAP * SUB // 2
BACK = 16 + CAP * SUB
ORDER = (2, 14, 4, 12, 6, 7, 10, 11, 8, 9, 5, 13, 0, 3, 15, 1)
GROUPS = NZ * NC
SELF = ORDER.index(0)
SELF_CHUNK = SELF * CHUNKS // GROUPS
NT = (((1,), (1,)), ((), ()))


def kernel(
    tok_hbm,
    cot_hbm,
    ids_ref,
    gate_ref,
    wg_hbm,
    wu_hbm,
    wd_hbm,
    home_hbm,
    ggrad_ref,
    slot_ref,
    src,
    wts,
    out_rows,
    in_rows,
    xrows,
    pre,
    grads,
    part,
    relay,
    full,
    ret_out,
    ret_in,
    home,
    load_sem,
    w_sem,
    disp_send,
    disp_recv,
    ag_send,
    ag_recv,
    rs_send,
    rs_recv,
    ret_send,
    ret_recv,
    out_sem,
):
    expert = lax.axis_index("expert")
    tensor = lax.axis_index("tensor")
    mz, mc = expert // NC, expert % NC
    my, mx = tensor // NX, tensor % NX

    def device(z, c, y, x):
        return (z * NC + c, y * NX + x)

    def each_peer(first, last, sign, act):
        def group(q, carry):
            code = jnp.int32(ORDER[0])
            for i in range(1, GROUPS):
                code = jnp.where(q == i, ORDER[i], code)
            z = lax.rem(mz + sign * (code // NC) + NZ, NZ)
            core = lax.rem(mc + code % NC, NC)
            for ky in range(NY):
                to = device(z, core, lax.rem(my + sign * ky + NY, NY), mx)
                k = q * NY + ky
                if ky == 0:
                    pl.when(q != SELF)(functools.partial(act, k, to))
                else:
                    act(k, to)
            return carry

        lax.fori_loop(first, last, group, 0)

    right = device(mz, mc, my, lax.rem(mx + 1, NX))
    left = device(mz, mc, my, lax.rem(mx + NX - 1, NX))

    loads = [
        pltpu.make_async_copy(tok_hbm, src.at[0], load_sem.at[0]),
        pltpu.make_async_copy(cot_hbm, src.at[1], load_sem.at[1]),
    ]
    weight_loads = [
        pltpu.make_async_copy(w.at[0], wts.at[i], w_sem.at[i])
        for i, w in enumerate((wg_hbm, wu_hbm, wd_hbm))
    ]
    for copy in loads + weight_loads:
        copy.start()

    barrier = pltpu.get_barrier_semaphore()

    def greet(k, to):
        pl.semaphore_signal(barrier, inc=1, device_id=to, device_id_type=MESH)

    each_peer(0, GROUPS, 1, greet)
    for neighbour in (left, right):
        pl.semaphore_signal(barrier, inc=1, device_id=neighbour, device_id_type=MESH)

    t0 = lax.broadcasted_iota(jnp.int32, (TOK, TOK), 0)
    t1 = lax.broadcasted_iota(jnp.int32, (TOK, TOK), 1)
    ids_row = ids_ref[...]
    ids = jnp.sum(jnp.where(t0 == t1, ids_row, 0), axis=1, keepdims=True)
    earlier = jnp.where((ids == ids_row) & (t1 < t0), 1, 0)
    position = jnp.sum(earlier, axis=1, keepdims=True)
    kz = ((ids >> 3) - mz) & (NZ - 1)
    kc = ((ids >> 2) - mc) & (NC - 1)
    ky = (ids - my) & (NY - 1)
    q_of = jnp.zeros_like(kz)
    for q in range(GROUPS):
        q_of = jnp.where(kz * NC + kc == ORDER[q], q, q_of)
    peer_of = q_of * NY + ky
    slot = peer_of * CAP + position
    slot_row = jnp.sum(jnp.where(t0 == t1, slot, 0), axis=0, keepdims=True)
    gate = jnp.sum(
        jnp.where(t0 == t1, gate_ref[...].astype(F32), 0.0), axis=1, keepdims=True
    )

    def columns(j):
        return pl.ds(pl.multiple_of(j * STEP, STEP), STEP)

    def tiles(j):
        return pl.ds(pl.multiple_of(j * (STEP // LANES), STEP // LANES), STEP // LANES)

    def sort(c, n):
        at = lax.broadcasted_iota(jnp.int32, (ROWS, TOK), 0) + c * ROWS
        pick = jnp.where(at == slot_row, 1.0, 0.0).astype(BF)
        for j in range(SPAN // STEP):
            cols = columns(n % SPLIT * (SPAN // STEP) + j)
            rows = jnp.dot(pick, src[n // SPLIT, :, cols], preferred_element_type=F32)
            out_rows[n, pl.ds(c * ROWS, ROWS), tiles(j), :] = pltpu.einshape(
                "a(bc)->abc", rows.astype(BF), c=LANES
            )

    def dispatch(c, n):

        def send(k, to):
            at = pl.ds(k * CAP, CAP)
            pltpu.make_async_remote_copy(
                src_ref=out_rows.at[n, at],
                dst_ref=in_rows.at[n, at],
                send_sem=disp_send.at[n, c],
                recv_sem=disp_recv.at[n, c],
                device_id=to,
                device_id_type=MESH,
            ).start()

        each_peer(c * GROUPS // CHUNKS, (c + 1) * GROUPS // CHUNKS, 1, send)

    def await_dispatch(c, n, sem):
        def wait(at):
            pltpu.make_async_copy(
                out_rows.at[n, at], in_rows.at[n, at], sem.at[n, c]
            ).wait()

        @pl.when(c == SELF_CHUNK)
        def _():
            wait(pl.ds(SELF_CHUNK * ROWS + CAP, ROWS - CAP))

        @pl.when(c != SELF_CHUNK)
        def _():
            wait(pl.ds(c * ROWS, ROWS))

    def gather_copy(c, n, kind):
        x = xrows.at[n // SPLIT, c]
        start = n % SPLIT * SPAN
        own, from_left, far, from_right = (pl.ds(i * ROWS, ROWS) for i in range(4))
        whole = pl.ds(start, SPAN)
        a, b = pl.ds(start, SPAN // 2), pl.ds(start + SPAN // 2, SPAN // 2)
        ref_pair, to = (
            ((x.at[own, whole], x.at[from_left, whole]), right),
            ((x.at[own, whole], x.at[from_right, whole]), left),
            ((x.at[from_left, a], x.at[far, a]), right),
            ((x.at[from_right, b], x.at[far, b]), left),
        )[kind]
        return pltpu.make_async_remote_copy(
            src_ref=ref_pair[0],
            dst_ref=ref_pair[1],
            send_sem=ag_send.at[n, c, kind],
            recv_sem=ag_recv.at[n, c, kind],
            device_id=to,
            device_id_type=MESH,
        )

    def arrive(c, h):
        for n in range(h * SPLIT, (h + 1) * SPLIT):
            await_dispatch(c, n, disp_recv)

            @pl.when(c == SELF_CHUNK)
            def _(n=n):
                at = slice(SELF_CHUNK * ROWS, SELF_CHUNK * ROWS + CAP)
                in_rows[n, at] = out_rows[n, at]

            for j in range(SPAN // STEP):
                cols = columns(n % SPLIT * (SPAN // STEP) + j)
                xrows[h, c, 0:ROWS, cols] = pltpu.einshape(
                    "abc->a(bc)", in_rows[n, pl.ds(c * ROWS, ROWS), tiles(j), :]
                )
            gather_copy(c, n, 0).start()
            gather_copy(c, n, 1).start()

    def forward(c, h):
        for n in range(h * SPLIT, (h + 1) * SPLIT):
            gather_copy(c, n, 0).wait_recv()
            gather_copy(c, n, 2).start()
            gather_copy(c, n, 1).wait_recv()
            gather_copy(c, n, 3).start()

    def project(c, h, w):
        pre[w] = jnp.zeros((MANY, HID), F32)

        def add(k, carry):
            at = pl.ds(pl.multiple_of(k * KTILE, KTILE), KTILE)
            pre[w] += lax.dot_general(
                xrows[h, c, :, at], wts[w, :, at], NT, preferred_element_type=F32
            )
            return carry

        lax.fori_loop(0, D // KTILE, add, 0)

    def compute(c, h):
        for n in range(h * SPLIT, (h + 1) * SPLIT):
            gather_copy(c, n, 2).wait_recv()
            gather_copy(c, n, 3).wait_recv()
        if h == 0:

            @pl.when(c == 0)
            def _():
                weight_loads[0].wait()
                weight_loads[1].wait()

            project(c, 0, 0)
            project(c, 0, 1)
            return

        @pl.when(c == 0)
        def _():
            weight_loads[2].wait()

        project(c, 1, 2)
        pre_gate, pre_up, d_hidden = pre[0], pre[1], pre[2]
        sigmoid_gate = jax.nn.sigmoid(pre_gate)
        swish_gate = pre_gate * sigmoid_gate
        hidden = (swish_gate * pre_up).astype(BF).astype(F32)
        gate_part = jnp.sum(hidden * d_hidden, axis=1, keepdims=True)
        part[c, :, 0:LANES] = jnp.broadcast_to(gate_part, (MANY, LANES)).astype(BF)
        d_gate = (
            d_hidden * pre_up * sigmoid_gate * (1.0 + pre_gate * (1.0 - sigmoid_gate))
        ).astype(BF)
        d_up = (d_hidden * swish_gate).astype(BF)
        grads[0] = d_gate
        grads[1] = d_up

        def unproject(k, carry):
            at = pl.ds(pl.multiple_of(k * NTILE, NTILE), NTILE)
            to = pl.ds(pl.multiple_of(LANES + k * NTILE, LANES), NTILE)
            part[c, :, to] = (
                jnp.dot(grads[0], wts[0, :, at], preferred_element_type=F32)
                + jnp.dot(grads[1], wts[1, :, at], preferred_element_type=F32)
            ).astype(BF)
            return carry

        for t in range(2):
            lax.fori_loop(
                t * HALF // NTILE, (t + 1) * HALF // NTILE, unproject, 0
            )
            for kind in range(4):
                scatter_copy(c, t, kind).start()

    def scatter_columns(t, side):
        start = LANES + t * HALF + side * HALF // 2
        return (0 if t == 0 and side == 0 else start), start + HALF // 2

    def scatter_copy(c, t, kind):
        p = part.at[c]
        from_left_rows, far, from_right_rows = (pl.ds(i * ROWS, ROWS) for i in (1, 2, 3))
        a, b = (pl.ds(i, j - i) for i, j in (scatter_columns(t, 0), scatter_columns(t, 1)))
        ref_pair, to = (
            ((p.at[far, a], relay.at[c, :, a]), right),
            ((p.at[far, b], relay.at[c, :, b]), left),
            ((p.at[from_right_rows, b], full.at[c, 0, :, b]), right),
            ((p.at[from_left_rows, a], full.at[c, 1, :, a]), left),
            ((p.at[from_right_rows, a], full.at[c, 0, :, a]), right),
            ((p.at[from_left_rows, b], full.at[c, 1, :, b]), left),
        )[kind]
        return pltpu.make_async_remote_copy(
            src_ref=ref_pair[0],
            dst_ref=ref_pair[1],
            send_sem=rs_send.at[c, t, kind],
            recv_sem=rs_recv.at[c, t, kind],
            device_id=to,
            device_id_type=MESH,
        )

    def pass_on(c, t):
        for kind, rows in ((0, slice(3 * ROWS, 4 * ROWS)), (1, slice(ROWS, 2 * ROWS))):
            scatter_copy(c, t, kind).wait_recv()
            cols = slice(*scatter_columns(t, kind))
            part[c, rows, cols] = (
                part[c, rows, cols].astype(F32) + relay[c, :, cols].astype(F32)
            ).astype(BF)
            scatter_copy(c, t, kind + 4).start()

    def send_home(c, t):
        for kind in (2, 3, 4, 5):
            scatter_copy(c, t, kind).wait_recv()

        def total(at):
            return (
                part[c, 0:ROWS, at].astype(F32)
                + full[c, 0, :, at].astype(F32)
                + full[c, 1, :, at].astype(F32)
            ).astype(BF)

        rows = pltpu.einshape(
            "a(bc)->abc", total(slice(LANES + t * HALF, LANES + (t + 1) * HALF)), c=LANES
        )
        ret_out[pl.ds(c * PER, PER), 16 + t * PIECE : 16 + (t + 1) * PIECE, :] = (
            rows.reshape(PER, PIECE, LANES)
        )
        if t == 0:
            r0 = lax.broadcasted_iota(jnp.int32, (PER * 16, ROWS), 0)
            r1 = lax.broadcasted_iota(jnp.int32, (PER * 16, ROWS), 1)
            spread = jnp.where(
                (r1 == (r0 >> 4) * CAP + (r0 & 15)) & ((r0 & 15) < CAP), 1.0, 0.0
            ).astype(BF)
            gates = jnp.dot(spread, total(slice(0, LANES)), preferred_element_type=F32)
            ret_out[pl.ds(c * PER, PER), 0:16, :] = gates.astype(BF).reshape(
                PER, 16, LANES
            )

        def send(k, to):
            pltpu.make_async_remote_copy(
                src_ref=ret_out.at[k, returned(t)],
                dst_ref=ret_in.at[k, returned(t)],
                send_sem=ret_send.at[c, t],
                recv_sem=ret_recv.at[c, t],
                device_id=to,
                device_id_type=MESH,
            ).start()

        each_peer(c * GROUPS // CHUNKS, (c + 1) * GROUPS // CHUNKS, -1, send)

        @pl.when(c == SELF_CHUNK)
        def _():
            ret_in[SELF_CHUNK * PER, returned(t)] = ret_out[SELF_CHUNK * PER, returned(t)]

    def returned(t):
        return pl.ds(0, 16 + PIECE) if t == 0 else pl.ds(16 + PIECE, PIECE)

    def await_return(c, t, sem):
        def wait(at):
            pltpu.make_async_copy(
                ret_out.at[at, returned(t)], ret_in.at[at, returned(t)], sem.at[c, t]
            ).wait()

        @pl.when(c == SELF_CHUNK)
        def _():
            wait(pl.ds(SELF_CHUNK * PER + 1, PER - 1))

        @pl.when(c != SELF_CHUNK)
        def _():
            wait(pl.ds(c * PER, PER))

    def home_copy(c):
        at = pl.ds(c * ROWS, ROWS)
        return pltpu.make_async_copy(home.at[at], home_hbm.at[at], out_sem.at[c])

    def come_home(c):
        for t in range(2):
            await_return(c, t, ret_recv)
            rows = ret_in[pl.ds(c * PER, PER), 16 + t * PIECE : 16 + (t + 1) * PIECE, :]
            home[pl.ds(c * ROWS, ROWS), t * HALF : (t + 1) * HALF] = pltpu.einshape(
                "abc->a(bc)", rows.reshape(ROWS, SUB // 2, LANES)
            )
        home_copy(c).start()

    def finish():
        at = lax.broadcasted_iota(jnp.int32, (TOK, PEERS * 16), 1)
        pick = jnp.where(at == peer_of * 16 + position, 1.0, 0.0).astype(BF)
        gates = jnp.dot(
            pick,
            ret_in[:, 0:16, :].reshape(PEERS * 16, LANES),
            preferred_element_type=F32,
        )
        ggrad = jnp.where(t0 == t1, gates / gate, 0.0)
        ggrad_ref[...] = jnp.sum(ggrad, axis=0, keepdims=True)
        slot_ref[...] = slot_row

    def drain():
        def ended(c, carry):
            for n in range(PIECES):
                await_dispatch(c, n, disp_send)
                for kind in range(4):
                    gather_copy(c, n, kind).wait_send()
            for t in range(2):
                for kind in range(6):
                    scatter_copy(c, t, kind).wait_send()
                await_return(c, t, ret_send)
            home_copy(c).wait()
            return carry

        lax.fori_loop(0, CHUNKS, ended, 0)

    def sd(c, h):
        def piece(n, carry):
            sort(c, n)
            dispatch(c, n)
            return carry

        lax.fori_loop(h * SPLIT, (h + 1) * SPLIT, piece, 0)

    loads[0].wait()
    sort(0, 0)
    pl.semaphore_wait(barrier, PEERS - 1 + 2)
    dispatch(0, 0)
    for n in range(1, SPLIT):
        sort(0, n)
        dispatch(0, n)
    loads[1].wait()
    for j in range(0, D, 1024):
        src[1, :, j : j + 1024] = (gate * src[1, :, j : j + 1024].astype(F32)).astype(BF)
    sd(0, 1)
    arrive(0, 0)
    sd(1, 0)
    sd(1, 1)
    arrive(0, 1)
    sd(2, 0)
    sd(2, 1)
    forward(0, 0)
    sd(3, 0)
    sd(3, 1)

    def step(c, carry):
        @pl.when(c < CHUNKS - 1)
        def _():
            arrive(c + 1, 0)

        forward(c, 1)
        compute(c, 0)

        @pl.when(c > 0)
        def _():
            pass_on(c - 1, 0)
            pass_on(c - 1, 1)

        @pl.when(c < CHUNKS - 1)
        def _():
            arrive(c + 1, 1)
            forward(c + 1, 0)

        compute(c, 1)

        @pl.when(c > 0)
        def _():
            send_home(c - 1, 0)
            send_home(c - 1, 1)

        return carry

    lax.fori_loop(0, CHUNKS, step, 0)
    pass_on(CHUNKS - 1, 0)
    pass_on(CHUNKS - 1, 1)
    lax.fori_loop(0, 2, lambda c, carry: come_home(c) or carry, 0)
    send_home(CHUNKS - 1, 0)
    send_home(CHUNKS - 1, 1)
    lax.fori_loop(2, CHUNKS, lambda c, carry: come_home(c) or carry, 0)
    finish()
    drain()


def unsort(home_ref, gate_ref, slot_ref, dtok_ref, ggrad_ref):
    t0 = lax.broadcasted_iota(jnp.int32, (TOK, TOK), 0)
    t1 = lax.broadcasted_iota(jnp.int32, (TOK, TOK), 1)
    slot = jnp.sum(jnp.where(t0 == t1, slot_ref[...], 0), axis=1, keepdims=True)
    at = lax.broadcasted_iota(jnp.int32, (TOK, SLOTS), 1)
    pick = jnp.where(at == slot, 1.0, 0.0).astype(BF)
    dtok_ref[...] = jnp.dot(pick, home_ref[...], preferred_element_type=F32).astype(BF)
    ggrad_ref[...] = gate_ref[...].astype(BF)


def local(tokens, cotangent, expert_ids, gate_values, gate_weight, up_weight, down_weight):
    vmem = pl.BlockSpec(memory_space=pltpu.VMEM)
    hbm = pl.BlockSpec(memory_space=pl.ANY)
    dma = pltpu.SemaphoreType.DMA
    home, gate_grad, slot = pl.pallas_call(
        kernel,
        out_shape=(
            jax.ShapeDtypeStruct((SLOTS, D), BF),
            jax.ShapeDtypeStruct((1, TOK), F32),
            jax.ShapeDtypeStruct((1, TOK), jnp.int32),
        ),
        in_specs=[hbm, hbm, vmem, vmem, hbm, hbm, hbm],
        out_specs=(hbm, vmem, vmem),
        scratch_shapes=[
            pltpu.VMEM((2, TOK, D), BF),
            pltpu.VMEM((3, HID, D), BF),
            pltpu.VMEM((PIECES, SLOTS, PSUB, LANES), BF),
            pltpu.VMEM((PIECES, SLOTS, PSUB, LANES), BF),
            pltpu.VMEM((2, CHUNKS, MANY, D), BF),
            pltpu.VMEM((3, MANY, HID), F32),
            pltpu.VMEM((2, MANY, HID), BF),
            pltpu.VMEM((CHUNKS, MANY, WIDE), BF),
            pltpu.VMEM((CHUNKS, ROWS, WIDE), BF),
            pltpu.VMEM((CHUNKS, 2, ROWS, WIDE), BF),
            pltpu.VMEM((PEERS, BACK, LANES), BF),
            pltpu.VMEM((PEERS, BACK, LANES), BF),
            pltpu.VMEM((SLOTS, D), BF),
            dma((2,)),
            dma((3,)),
            dma((PIECES, CHUNKS)),
            dma((PIECES, CHUNKS)),
            dma((PIECES, CHUNKS, 4)),
            dma((PIECES, CHUNKS, 4)),
            dma((CHUNKS, 2, 6)),
            dma((CHUNKS, 2, 6)),
            dma((CHUNKS, 2)),
            dma((CHUNKS, 2)),
            dma((CHUNKS,)),
        ],
        compiler_params=pltpu.CompilerParams(
            collective_id=0, has_side_effects=True, vmem_limit_bytes=60 * 2**20
        ),
    )(
        tokens,
        cotangent,
        expert_ids.reshape(1, TOK),
        gate_values.reshape(1, TOK),
        gate_weight,
        up_weight,
        down_weight,
    )
    d_tokens, gate_grad = pl.pallas_call(
        unsort,
        grid=(D // UNSORT,),
        out_shape=(
            jax.ShapeDtypeStruct((TOK, D), BF),
            jax.ShapeDtypeStruct((1, TOK), BF),
        ),
        in_specs=[
            pl.BlockSpec((SLOTS, UNSORT), lambda j: (0, j)),
            pl.BlockSpec((1, TOK), lambda j: (0, 0)),
            pl.BlockSpec((1, TOK), lambda j: (0, 0)),
        ],
        out_specs=(
            pl.BlockSpec((TOK, UNSORT), lambda j: (0, j)),
            pl.BlockSpec((1, TOK), lambda j: (0, 0)),
        ),
    )(home, gate_grad, slot)
    return d_tokens, gate_grad.reshape(TOK, 1)


def solution(mesh):
    rows = P(("expert", "tensor"), None)
    blocks = P(("expert", "tensor"), None, None)
    return jax.shard_map(
        local,
        mesh=mesh,
        in_specs=(rows, rows, rows, rows, blocks, blocks, blocks),
        out_specs=(rows, rows),
        check_vma=False,
    )
```

```python
import functools

import jax
import jax.numpy as jnp
from jax import lax
from jax.experimental import pallas as pl
from jax.experimental.pallas import tpu as pltpu
from jax.sharding import PartitionSpec as P

MESH = pl.DeviceIdType.MESH
BF = jnp.bfloat16
F32 = jnp.float32

D = 4096
HID = 384
TOK = 128
CAP = 3
NZ, NY, NC, NX = 8, 4, 2, 4
PEERS = NZ * NY * NC
SLOTS = PEERS * CAP
CHUNKS = 4
PER = PEERS // CHUNKS
ROWS = PER * CAP
MANY = ROWS * NX
LANES = 128
SUB = D // LANES
WIDE = LANES + D
HALF = D // 2
KTILE = 1024
NTILE = 512
SPLIT = 2
PIECES = 2 * SPLIT
SPAN = D // SPLIT
PSUB = SPAN // LANES
STEP = 2048
UNSORT = 2048
PIECE = CAP * SUB // 2
BACK = 16 + CAP * SUB
ORDER = (2, 14, 4, 12, 6, 10, 7, 11, 8, 9, 3, 15, 0, 5, 13, 1)
GROUPS = NZ * NC
SELF = ORDER.index(0)
SELF_CHUNK = SELF * CHUNKS // GROUPS
NT = (((1,), (1,)), ((), ()))


def kernel(
    tok_hbm,
    cot_hbm,
    ids_ref,
    gate_ref,
    wg_hbm,
    wu_hbm,
    wd_hbm,
    home_hbm,
    ggrad_ref,
    slot_ref,
    src,
    wts,
    out_rows,
    in_rows,
    xrows,
    pre,
    grads,
    part,
    relay,
    full,
    ret_out,
    ret_in,
    home,
    load_sem,
    w_sem,
    disp_send,
    disp_recv,
    ag_send,
    ag_recv,
    rs_send,
    rs_recv,
    ret_send,
    ret_recv,
    out_sem,
):
    expert = lax.axis_index("expert")
    tensor = lax.axis_index("tensor")
    mz, mc = expert // NC, expert % NC
    my, mx = tensor // NX, tensor % NX

    def device(z, c, y, x):
        return (z * NC + c, y * NX + x)

    def each_peer(first, last, sign, act):
        def group(q, carry):
            code = jnp.int32(ORDER[0])
            for i in range(1, GROUPS):
                code = jnp.where(q == i, ORDER[i], code)
            z = lax.rem(mz + sign * (code // NC) + NZ, NZ)
            core = lax.rem(mc + code % NC, NC)
            for ky in range(NY):
                to = device(z, core, lax.rem(my + sign * ky + NY, NY), mx)
                k = q * NY + ky
                if ky == 0:
                    pl.when(q != SELF)(functools.partial(act, k, to))
                else:
                    act(k, to)
            return carry

        lax.fori_loop(first, last, group, 0)

    right = device(mz, mc, my, lax.rem(mx + 1, NX))
    left = device(mz, mc, my, lax.rem(mx + NX - 1, NX))

    loads = [
        pltpu.make_async_copy(tok_hbm, src.at[0], load_sem.at[0]),
        pltpu.make_async_copy(cot_hbm, src.at[1], load_sem.at[1]),
    ]
    weight_loads = [
        pltpu.make_async_copy(w.at[0], wts.at[i], w_sem.at[i])
        for i, w in enumerate((wg_hbm, wu_hbm, wd_hbm))
    ]
    for copy in loads + weight_loads:
        copy.start()

    barrier = pltpu.get_barrier_semaphore()

    def greet(k, to):
        pl.semaphore_signal(barrier, inc=1, device_id=to, device_id_type=MESH)

    each_peer(0, GROUPS, 1, greet)
    for neighbour in (left, right):
        pl.semaphore_signal(barrier, inc=1, device_id=neighbour, device_id_type=MESH)

    t0 = lax.broadcasted_iota(jnp.int32, (TOK, TOK), 0)
    t1 = lax.broadcasted_iota(jnp.int32, (TOK, TOK), 1)
    ids_row = ids_ref[...]
    ids = jnp.sum(jnp.where(t0 == t1, ids_row, 0), axis=1, keepdims=True)
    earlier = jnp.where((ids == ids_row) & (t1 < t0), 1, 0)
    position = jnp.sum(earlier, axis=1, keepdims=True)
    kz = ((ids >> 3) - mz) & (NZ - 1)
    kc = ((ids >> 2) - mc) & (NC - 1)
    ky = (ids - my) & (NY - 1)
    q_of = jnp.zeros_like(kz)
    for q in range(GROUPS):
        q_of = jnp.where(kz * NC + kc == ORDER[q], q, q_of)
    peer_of = q_of * NY + ky
    slot = peer_of * CAP + position
    slot_row = jnp.sum(jnp.where(t0 == t1, slot, 0), axis=0, keepdims=True)
    gate = jnp.sum(
        jnp.where(t0 == t1, gate_ref[...].astype(F32), 0.0), axis=1, keepdims=True
    )

    def columns(j):
        return pl.ds(pl.multiple_of(j * STEP, STEP), STEP)

    def tiles(j):
        return pl.ds(pl.multiple_of(j * (STEP // LANES), STEP // LANES), STEP // LANES)

    def sort(c, n):
        at = lax.broadcasted_iota(jnp.int32, (ROWS, TOK), 0) + c * ROWS
        pick = jnp.where(at == slot_row, 1.0, 0.0).astype(BF)
        for j in range(SPAN // STEP):
            cols = columns(n % SPLIT * (SPAN // STEP) + j)
            rows = jnp.dot(pick, src[n // SPLIT, :, cols], preferred_element_type=F32)
            out_rows[n, pl.ds(c * ROWS, ROWS), tiles(j), :] = pltpu.einshape(
                "a(bc)->abc", rows.astype(BF), c=LANES
            )

    def dispatch(c, n):

        def send(k, to):
            at = pl.ds(k * CAP, CAP)
            pltpu.make_async_remote_copy(
                src_ref=out_rows.at[n, at],
                dst_ref=in_rows.at[n, at],
                send_sem=disp_send.at[n, c],
                recv_sem=disp_recv.at[n, c],
                device_id=to,
                device_id_type=MESH,
            ).start()

        each_peer(c * GROUPS // CHUNKS, (c + 1) * GROUPS // CHUNKS, 1, send)

    def await_dispatch(c, n, sem):
        def wait(at):
            pltpu.make_async_copy(
                out_rows.at[n, at], in_rows.at[n, at], sem.at[n, c]
            ).wait()

        @pl.when(c == SELF_CHUNK)
        def _():
            wait(pl.ds(SELF_CHUNK * ROWS + CAP, ROWS - CAP))

        @pl.when(c != SELF_CHUNK)
        def _():
            wait(pl.ds(c * ROWS, ROWS))

    def gather_copy(c, n, kind):
        x = xrows.at[n // SPLIT, c]
        start = n % SPLIT * SPAN
        own, from_left, far, from_right = (pl.ds(i * ROWS, ROWS) for i in range(4))
        whole = pl.ds(start, SPAN)
        a, b = pl.ds(start, SPAN // 2), pl.ds(start + SPAN // 2, SPAN // 2)
        ref_pair, to = (
            ((x.at[own, whole], x.at[from_left, whole]), right),
            ((x.at[own, whole], x.at[from_right, whole]), left),
            ((x.at[from_left, a], x.at[far, a]), right),
            ((x.at[from_right, b], x.at[far, b]), left),
        )[kind]
        return pltpu.make_async_remote_copy(
            src_ref=ref_pair[0],
            dst_ref=ref_pair[1],
            send_sem=ag_send.at[n, c, kind],
            recv_sem=ag_recv.at[n, c, kind],
            device_id=to,
            device_id_type=MESH,
        )

    def arrive(c, h):
        for n in range(h * SPLIT, (h + 1) * SPLIT):
            await_dispatch(c, n, disp_recv)

            @pl.when(c == SELF_CHUNK)
            def _(n=n):
                at = slice(SELF_CHUNK * ROWS, SELF_CHUNK * ROWS + CAP)
                in_rows[n, at] = out_rows[n, at]

            for j in range(SPAN // STEP):
                cols = columns(n % SPLIT * (SPAN // STEP) + j)
                xrows[h, c, 0:ROWS, cols] = pltpu.einshape(
                    "abc->a(bc)", in_rows[n, pl.ds(c * ROWS, ROWS), tiles(j), :]
                )
            gather_copy(c, n, 0).start()
            gather_copy(c, n, 1).start()

    def forward(c, h):
        for n in range(h * SPLIT, (h + 1) * SPLIT):
            gather_copy(c, n, 0).wait_recv()
            gather_copy(c, n, 2).start()
            gather_copy(c, n, 1).wait_recv()
            gather_copy(c, n, 3).start()

    def project(c, h, ws):
        for w in ws:
            pre[w] = jnp.zeros((MANY, HID), F32)

        def add(k, carry):
            at = pl.ds(pl.multiple_of(k * KTILE, KTILE), KTILE)
            for w in ws:
                pre[w] += lax.dot_general(
                    xrows[h, c, :, at], wts[w, :, at], NT, preferred_element_type=F32
                )
            return carry

        for i in range(SPLIT):
            n = h * SPLIT + i
            gather_copy(c, n, 2).wait_recv()
            gather_copy(c, n, 3).wait_recv()
            lax.fori_loop(i * SPAN // KTILE, (i + 1) * SPAN // KTILE, add, 0)

    def compute(c, h):
        if h == 0:

            @pl.when(c == 0)
            def _():
                weight_loads[0].wait()
                weight_loads[1].wait()

            project(c, 0, (0, 1))
            return

        @pl.when(c == 0)
        def _():
            weight_loads[2].wait()

        project(c, 1, (2,))
        pre_gate, pre_up, d_hidden = pre[0], pre[1], pre[2]
        sigmoid_gate = jax.nn.sigmoid(pre_gate)
        swish_gate = pre_gate * sigmoid_gate
        hidden = (swish_gate * pre_up).astype(BF).astype(F32)
        gate_part = jnp.sum(hidden * d_hidden, axis=1, keepdims=True)
        part[c, :, 0:LANES] = jnp.broadcast_to(gate_part, (MANY, LANES)).astype(BF)
        d_gate = (
            d_hidden * pre_up * sigmoid_gate * (1.0 + pre_gate * (1.0 - sigmoid_gate))
        ).astype(BF)
        d_up = (d_hidden * swish_gate).astype(BF)
        grads[0] = d_gate
        grads[1] = d_up

        def unproject(k, carry):
            at = pl.ds(pl.multiple_of(k * NTILE, NTILE), NTILE)
            to = pl.ds(pl.multiple_of(LANES + k * NTILE, LANES), NTILE)
            part[c, :, to] = (
                jnp.dot(grads[0], wts[0, :, at], preferred_element_type=F32)
                + jnp.dot(grads[1], wts[1, :, at], preferred_element_type=F32)
            ).astype(BF)
            return carry

        for t in range(2):
            lax.fori_loop(
                t * HALF // NTILE, (t + 1) * HALF // NTILE, unproject, 0
            )
            for kind in range(4):
                scatter_copy(c, t, kind).start()

    def scatter_columns(t, side):
        start = LANES + t * HALF + side * HALF // 2
        return (0 if t == 0 and side == 0 else start), start + HALF // 2

    def scatter_copy(c, t, kind):
        p = part.at[c]
        from_left_rows, far, from_right_rows = (pl.ds(i * ROWS, ROWS) for i in (1, 2, 3))
        a, b = (pl.ds(i, j - i) for i, j in (scatter_columns(t, 0), scatter_columns(t, 1)))
        ref_pair, to = (
            ((p.at[far, a], relay.at[c, :, a]), right),
            ((p.at[far, b], relay.at[c, :, b]), left),
            ((p.at[from_right_rows, b], full.at[c, 0, :, b]), right),
            ((p.at[from_left_rows, a], full.at[c, 1, :, a]), left),
            ((p.at[from_right_rows, a], full.at[c, 0, :, a]), right),
            ((p.at[from_left_rows, b], full.at[c, 1, :, b]), left),
        )[kind]
        return pltpu.make_async_remote_copy(
            src_ref=ref_pair[0],
            dst_ref=ref_pair[1],
            send_sem=rs_send.at[c, t, kind],
            recv_sem=rs_recv.at[c, t, kind],
            device_id=to,
            device_id_type=MESH,
        )

    def pass_on(c, t):
        for kind, rows in ((0, slice(3 * ROWS, 4 * ROWS)), (1, slice(ROWS, 2 * ROWS))):
            scatter_copy(c, t, kind).wait_recv()
            cols = slice(*scatter_columns(t, kind))
            part[c, rows, cols] = (
                part[c, rows, cols].astype(F32) + relay[c, :, cols].astype(F32)
            ).astype(BF)
            scatter_copy(c, t, kind + 4).start()

    def send_home(c, t):
        for kind in (2, 3, 4, 5):
            scatter_copy(c, t, kind).wait_recv()

        def total(at):
            return (
                part[c, 0:ROWS, at].astype(F32)
                + full[c, 0, :, at].astype(F32)
                + full[c, 1, :, at].astype(F32)
            ).astype(BF)

        rows = pltpu.einshape(
            "a(bc)->abc", total(slice(LANES + t * HALF, LANES + (t + 1) * HALF)), c=LANES
        )
        ret_out[pl.ds(c * PER, PER), 16 + t * PIECE : 16 + (t + 1) * PIECE, :] = (
            rows.reshape(PER, PIECE, LANES)
        )
        if t == 0:
            r0 = lax.broadcasted_iota(jnp.int32, (PER * 16, ROWS), 0)
            r1 = lax.broadcasted_iota(jnp.int32, (PER * 16, ROWS), 1)
            spread = jnp.where(
                (r1 == (r0 >> 4) * CAP + (r0 & 15)) & ((r0 & 15) < CAP), 1.0, 0.0
            ).astype(BF)
            gates = jnp.dot(spread, total(slice(0, LANES)), preferred_element_type=F32)
            ret_out[pl.ds(c * PER, PER), 0:16, :] = gates.astype(BF).reshape(
                PER, 16, LANES
            )

        def send(k, to):
            pltpu.make_async_remote_copy(
                src_ref=ret_out.at[k, returned(t)],
                dst_ref=ret_in.at[k, returned(t)],
                send_sem=ret_send.at[c, t],
                recv_sem=ret_recv.at[c, t],
                device_id=to,
                device_id_type=MESH,
            ).start()

        each_peer(c * GROUPS // CHUNKS, (c + 1) * GROUPS // CHUNKS, -1, send)

        @pl.when(c == SELF_CHUNK)
        def _():
            ret_in[SELF_CHUNK * PER, returned(t)] = ret_out[SELF_CHUNK * PER, returned(t)]

    def returned(t):
        return pl.ds(0, 16 + PIECE) if t == 0 else pl.ds(16 + PIECE, PIECE)

    def await_return(c, t, sem):
        def wait(at):
            pltpu.make_async_copy(
                ret_out.at[at, returned(t)], ret_in.at[at, returned(t)], sem.at[c, t]
            ).wait()

        @pl.when(c == SELF_CHUNK)
        def _():
            wait(pl.ds(SELF_CHUNK * PER + 1, PER - 1))

        @pl.when(c != SELF_CHUNK)
        def _():
            wait(pl.ds(c * PER, PER))

    def home_copy(c):
        at = pl.ds(c * ROWS, ROWS)
        return pltpu.make_async_copy(home.at[at], home_hbm.at[at], out_sem.at[c])

    def come_home(c):
        for t in range(2):
            await_return(c, t, ret_recv)
            rows = ret_in[pl.ds(c * PER, PER), 16 + t * PIECE : 16 + (t + 1) * PIECE, :]
            home[pl.ds(c * ROWS, ROWS), t * HALF : (t + 1) * HALF] = pltpu.einshape(
                "abc->a(bc)", rows.reshape(ROWS, SUB // 2, LANES)
            )
        home_copy(c).start()

    def finish():
        at = lax.broadcasted_iota(jnp.int32, (TOK, PEERS * 16), 1)
        pick = jnp.where(at == peer_of * 16 + position, 1.0, 0.0).astype(BF)
        gates = jnp.dot(
            pick,
            ret_in[:, 0:16, :].reshape(PEERS * 16, LANES),
            preferred_element_type=F32,
        )
        ggrad = jnp.where(t0 == t1, gates / gate, 0.0)
        ggrad_ref[...] = jnp.sum(ggrad, axis=0, keepdims=True)
        slot_ref[...] = slot_row

    def drain():
        def ended(c, carry):
            for n in range(PIECES):
                await_dispatch(c, n, disp_send)
                for kind in range(4):
                    gather_copy(c, n, kind).wait_send()
            for t in range(2):
                for kind in range(6):
                    scatter_copy(c, t, kind).wait_send()
                await_return(c, t, ret_send)
            home_copy(c).wait()
            return carry

        lax.fori_loop(0, CHUNKS, ended, 0)

    def sd(c, h):
        def piece(n, carry):
            sort(c, n)
            dispatch(c, n)
            return carry

        lax.fori_loop(h * SPLIT, (h + 1) * SPLIT, piece, 0)

    loads[0].wait()
    sort(0, 0)
    pl.semaphore_wait(barrier, PEERS - 1 + 2)
    dispatch(0, 0)
    for n in range(1, SPLIT):
        sort(0, n)
        dispatch(0, n)
    loads[1].wait()
    for j in range(0, D, 1024):
        src[1, :, j : j + 1024] = (gate * src[1, :, j : j + 1024].astype(F32)).astype(BF)
    sd(0, 1)
    arrive(0, 0)
    sd(1, 0)
    sd(1, 1)
    arrive(0, 1)
    sd(2, 0)
    sd(2, 1)
    forward(0, 0)
    sd(3, 0)
    sd(3, 1)

    def step(c, carry):
        @pl.when(c < CHUNKS - 1)
        def _():
            arrive(c + 1, 0)

        forward(c, 1)
        compute(c, 0)

        @pl.when(c > 0)
        def _():
            pass_on(c - 1, 0)
            pass_on(c - 1, 1)

        @pl.when(c < CHUNKS - 1)
        def _():
            arrive(c + 1, 1)
            forward(c + 1, 0)

        compute(c, 1)

        @pl.when(c > 0)
        def _():
            send_home(c - 1, 0)
            send_home(c - 1, 1)

        return carry

    lax.fori_loop(0, CHUNKS, step, 0)
    pass_on(CHUNKS - 1, 0)
    pass_on(CHUNKS - 1, 1)
    lax.fori_loop(0, 2, lambda c, carry: come_home(c) or carry, 0)
    send_home(CHUNKS - 1, 0)
    send_home(CHUNKS - 1, 1)
    lax.fori_loop(2, CHUNKS, lambda c, carry: come_home(c) or carry, 0)
    finish()
    drain()


def unsort(home_ref, gate_ref, slot_ref, dtok_ref, ggrad_ref):
    t0 = lax.broadcasted_iota(jnp.int32, (TOK, TOK), 0)
    t1 = lax.broadcasted_iota(jnp.int32, (TOK, TOK), 1)
    slot = jnp.sum(jnp.where(t0 == t1, slot_ref[...], 0), axis=1, keepdims=True)
    at = lax.broadcasted_iota(jnp.int32, (TOK, SLOTS), 1)
    pick = jnp.where(at == slot, 1.0, 0.0).astype(BF)
    dtok_ref[...] = jnp.dot(pick, home_ref[...], preferred_element_type=F32).astype(BF)
    ggrad_ref[...] = gate_ref[...].astype(BF)


def local(tokens, cotangent, expert_ids, gate_values, gate_weight, up_weight, down_weight):
    vmem = pl.BlockSpec(memory_space=pltpu.VMEM)
    hbm = pl.BlockSpec(memory_space=pl.ANY)
    dma = pltpu.SemaphoreType.DMA
    home, gate_grad, slot = pl.pallas_call(
        kernel,
        out_shape=(
            jax.ShapeDtypeStruct((SLOTS, D), BF),
            jax.ShapeDtypeStruct((1, TOK), F32),
            jax.ShapeDtypeStruct((1, TOK), jnp.int32),
        ),
        in_specs=[hbm, hbm, vmem, vmem, hbm, hbm, hbm],
        out_specs=(hbm, vmem, vmem),
        scratch_shapes=[
            pltpu.VMEM((2, TOK, D), BF),
            pltpu.VMEM((3, HID, D), BF),
            pltpu.VMEM((PIECES, SLOTS, PSUB, LANES), BF),
            pltpu.VMEM((PIECES, SLOTS, PSUB, LANES), BF),
            pltpu.VMEM((2, CHUNKS, MANY, D), BF),
            pltpu.VMEM((3, MANY, HID), F32),
            pltpu.VMEM((2, MANY, HID), BF),
            pltpu.VMEM((CHUNKS, MANY, WIDE), BF),
            pltpu.VMEM((CHUNKS, ROWS, WIDE), BF),
            pltpu.VMEM((CHUNKS, 2, ROWS, WIDE), BF),
            pltpu.VMEM((PEERS, BACK, LANES), BF),
            pltpu.VMEM((PEERS, BACK, LANES), BF),
            pltpu.VMEM((SLOTS, D), BF),
            dma((2,)),
            dma((3,)),
            dma((PIECES, CHUNKS)),
            dma((PIECES, CHUNKS)),
            dma((PIECES, CHUNKS, 4)),
            dma((PIECES, CHUNKS, 4)),
            dma((CHUNKS, 2, 6)),
            dma((CHUNKS, 2, 6)),
            dma((CHUNKS, 2)),
            dma((CHUNKS, 2)),
            dma((CHUNKS,)),
        ],
        compiler_params=pltpu.CompilerParams(
            collective_id=0, has_side_effects=True, vmem_limit_bytes=60 * 2**20
        ),
    )(
        tokens,
        cotangent,
        expert_ids.reshape(1, TOK),
        gate_values.reshape(1, TOK),
        gate_weight,
        up_weight,
        down_weight,
    )
    d_tokens, gate_grad = pl.pallas_call(
        unsort,
        grid=(D // UNSORT,),
        out_shape=(
            jax.ShapeDtypeStruct((TOK, D), BF),
            jax.ShapeDtypeStruct((1, TOK), BF),
        ),
        in_specs=[
            pl.BlockSpec((SLOTS, UNSORT), lambda j: (0, j)),
            pl.BlockSpec((1, TOK), lambda j: (0, 0)),
            pl.BlockSpec((1, TOK), lambda j: (0, 0)),
        ],
        out_specs=(
            pl.BlockSpec((TOK, UNSORT), lambda j: (0, j)),
            pl.BlockSpec((1, TOK), lambda j: (0, 0)),
        ),
    )(home, gate_grad, slot)
    return d_tokens, gate_grad.reshape(TOK, 1)


def solution(mesh):
    rows = P(("expert", "tensor"), None)
    blocks = P(("expert", "tensor"), None, None)
    return jax.shard_map(
        local,
        mesh=mesh,
        in_specs=(rows, rows, rows, rows, blocks, blocks, blocks),
        out_specs=(rows, rows),
        check_vma=False,
    )
```

```python
import functools

import jax
import jax.numpy as jnp
from jax import lax
from jax.experimental import pallas as pl
from jax.experimental.pallas import tpu as pltpu
from jax.sharding import PartitionSpec as P

MESH = pl.DeviceIdType.MESH
BF = jnp.bfloat16
F32 = jnp.float32

D = 4096
HID = 384
TOK = 128
CAP = 3
NZ, NY, NC, NX = 8, 4, 2, 4
PEERS = NZ * NY * NC
SLOTS = PEERS * CAP
CHUNKS = 4
PER = PEERS // CHUNKS
ROWS = PER * CAP
MANY = ROWS * NX
LANES = 128
SUB = D // LANES
WIDE = LANES + D
HALF = D // 2
KTILE = 1024
NTILE = 512
SPLIT = 2
PIECES = 2 * SPLIT
SPAN = D // SPLIT
PSUB = SPAN // LANES
STEP = 2048
UNSORT = 2048
PIECE = CAP * SUB // 2
BACK = 16 + CAP * SUB
ORDER = (2, 14, 4, 12, 6, 10, 7, 11, 8, 9, 3, 15, 0, 5, 13, 1)
GROUPS = NZ * NC
SELF = ORDER.index(0)
SELF_CHUNK = SELF * CHUNKS // GROUPS
NT = (((1,), (1,)), ((), ()))


def kernel(
    tok_hbm,
    cot_hbm,
    ids_ref,
    gate_ref,
    wg_hbm,
    wu_hbm,
    wd_hbm,
    home_hbm,
    ggrad_ref,
    slot_ref,
    src,
    wts,
    out_rows,
    in_rows,
    xrows,
    pre,
    grads,
    part,
    relay,
    full,
    ret_out,
    ret_in,
    home,
    load_sem,
    w_sem,
    disp_send,
    disp_recv,
    ag_send,
    ag_recv,
    rs_send,
    rs_recv,
    ret_send,
    ret_recv,
    out_sem,
):
    expert = lax.axis_index("expert")
    tensor = lax.axis_index("tensor")
    mz, mc = expert // NC, expert % NC
    my, mx = tensor // NX, tensor % NX

    def device(z, c, y, x):
        return (z * NC + c, y * NX + x)

    def each_peer(first, last, sign, act):
        def group(q, carry):
            code = jnp.int32(ORDER[0])
            for i in range(1, GROUPS):
                code = jnp.where(q == i, ORDER[i], code)
            z = lax.rem(mz + sign * (code // NC) + NZ, NZ)
            core = lax.rem(mc + code % NC, NC)
            for ky in range(NY):
                to = device(z, core, lax.rem(my + sign * ky + NY, NY), mx)
                k = q * NY + ky
                if ky == 0:
                    pl.when(q != SELF)(functools.partial(act, k, to))
                else:
                    act(k, to)
            return carry

        lax.fori_loop(first, last, group, 0)

    right = device(mz, mc, my, lax.rem(mx + 1, NX))
    left = device(mz, mc, my, lax.rem(mx + NX - 1, NX))

    loads = [
        pltpu.make_async_copy(tok_hbm, src.at[0], load_sem.at[0]),
        pltpu.make_async_copy(cot_hbm, src.at[1], load_sem.at[1]),
    ]
    weight_loads = [
        pltpu.make_async_copy(w.at[0], wts.at[i], w_sem.at[i])
        for i, w in enumerate((wg_hbm, wu_hbm, wd_hbm))
    ]
    for copy in loads + weight_loads:
        copy.start()

    barrier = pltpu.get_barrier_semaphore()

    def greet(k, to):
        pl.semaphore_signal(barrier, inc=1, device_id=to, device_id_type=MESH)

    each_peer(0, GROUPS, 1, greet)
    for neighbour in (left, right):
        pl.semaphore_signal(barrier, inc=1, device_id=neighbour, device_id_type=MESH)

    t0 = lax.broadcasted_iota(jnp.int32, (TOK, TOK), 0)
    t1 = lax.broadcasted_iota(jnp.int32, (TOK, TOK), 1)
    ids_row = ids_ref[...]
    ids = jnp.sum(jnp.where(t0 == t1, ids_row, 0), axis=1, keepdims=True)
    earlier = jnp.where((ids == ids_row) & (t1 < t0), 1, 0)
    position = jnp.sum(earlier, axis=1, keepdims=True)
    kz = ((ids >> 3) - mz) & (NZ - 1)
    kc = ((ids >> 2) - mc) & (NC - 1)
    ky = (ids - my) & (NY - 1)
    q_of = jnp.zeros_like(kz)
    for q in range(GROUPS):
        q_of = jnp.where(kz * NC + kc == ORDER[q], q, q_of)
    peer_of = q_of * NY + ky
    slot = peer_of * CAP + position
    slot_row = jnp.sum(jnp.where(t0 == t1, slot, 0), axis=0, keepdims=True)
    gate = jnp.sum(
        jnp.where(t0 == t1, gate_ref[...].astype(F32), 0.0), axis=1, keepdims=True
    )

    def columns(j):
        return pl.ds(pl.multiple_of(j * STEP, STEP), STEP)

    def tiles(j):
        return pl.ds(pl.multiple_of(j * (STEP // LANES), STEP // LANES), STEP // LANES)

    def sort(c, n):
        at = lax.broadcasted_iota(jnp.int32, (ROWS, TOK), 0) + c * ROWS
        pick = jnp.where(at == slot_row, 1.0, 0.0).astype(BF)
        for j in range(SPAN // STEP):
            cols = columns(n % SPLIT * (SPAN // STEP) + j)
            rows = jnp.dot(pick, src[n // SPLIT, :, cols], preferred_element_type=F32)
            out_rows[n, pl.ds(c * ROWS, ROWS), tiles(j), :] = pltpu.einshape(
                "a(bc)->abc", rows.astype(BF), c=LANES
            )

    def dispatch(c, n):

        def send(k, to):
            at = pl.ds(k * CAP, CAP)
            pltpu.make_async_remote_copy(
                src_ref=out_rows.at[n, at],
                dst_ref=in_rows.at[n, at],
                send_sem=disp_send.at[n, c],
                recv_sem=disp_recv.at[n, c],
                device_id=to,
                device_id_type=MESH,
            ).start()

        each_peer(c * GROUPS // CHUNKS, (c + 1) * GROUPS // CHUNKS, 1, send)

    def await_dispatch(c, n, sem):
        def wait(at):
            pltpu.make_async_copy(
                out_rows.at[n, at], in_rows.at[n, at], sem.at[n, c]
            ).wait()

        @pl.when(c == SELF_CHUNK)
        def _():
            wait(pl.ds(SELF_CHUNK * ROWS + CAP, ROWS - CAP))

        @pl.when(c != SELF_CHUNK)
        def _():
            wait(pl.ds(c * ROWS, ROWS))

    def gather_copy(c, n, kind):
        x = xrows.at[n // SPLIT, c]
        start = n % SPLIT * SPAN
        own, from_left, far, from_right = (pl.ds(i * ROWS, ROWS) for i in range(4))
        whole = pl.ds(start, SPAN)
        a, b = pl.ds(start, SPAN // 2), pl.ds(start + SPAN // 2, SPAN // 2)
        ref_pair, to = (
            ((x.at[own, whole], x.at[from_left, whole]), right),
            ((x.at[own, whole], x.at[from_right, whole]), left),
            ((x.at[from_left, a], x.at[far, a]), right),
            ((x.at[from_right, b], x.at[far, b]), left),
        )[kind]
        return pltpu.make_async_remote_copy(
            src_ref=ref_pair[0],
            dst_ref=ref_pair[1],
            send_sem=ag_send.at[n, c, kind],
            recv_sem=ag_recv.at[n, c, kind],
            device_id=to,
            device_id_type=MESH,
        )

    def arrive(c, h):
        for n in range(h * SPLIT, (h + 1) * SPLIT):
            await_dispatch(c, n, disp_recv)

            @pl.when(c == SELF_CHUNK)
            def _(n=n):
                at = slice(SELF_CHUNK * ROWS, SELF_CHUNK * ROWS + CAP)
                in_rows[n, at] = out_rows[n, at]

            for j in range(SPAN // STEP):
                cols = columns(n % SPLIT * (SPAN // STEP) + j)
                xrows[h, c, 0:ROWS, cols] = pltpu.einshape(
                    "abc->a(bc)", in_rows[n, pl.ds(c * ROWS, ROWS), tiles(j), :]
                )
            gather_copy(c, n, 0).start()
            gather_copy(c, n, 1).start()

    def forward(c, h):
        for n in range(h * SPLIT, (h + 1) * SPLIT):
            gather_copy(c, n, 0).wait_recv()
            gather_copy(c, n, 2).start()
            gather_copy(c, n, 1).wait_recv()
            gather_copy(c, n, 3).start()

    def project(c, h, ws):
        for w in ws:
            pre[w] = jnp.zeros((MANY, HID), F32)

        def add(k, carry):
            at = pl.ds(pl.multiple_of(k * KTILE, KTILE), KTILE)
            for w in ws:
                pre[w] += lax.dot_general(
                    xrows[h, c, :, at], wts[w, :, at], NT, preferred_element_type=F32
                )
            return carry

        for i in range(SPLIT):
            n = h * SPLIT + i
            gather_copy(c, n, 2).wait_recv()
            gather_copy(c, n, 3).wait_recv()
            lax.fori_loop(i * SPAN // KTILE, (i + 1) * SPAN // KTILE, add, 0)

    def compute(c, h):
        if h == 0:

            @pl.when(c == 0)
            def _():
                weight_loads[0].wait()
                weight_loads[1].wait()

            project(c, 0, (0, 1))
            pre_gate, pre_up = pre[0], pre[1]
            sigmoid_gate = jax.nn.sigmoid(pre_gate)
            swish_gate = pre_gate * sigmoid_gate
            pre[3] = (swish_gate * pre_up).astype(BF).astype(F32)
            pre[0] = pre_up * sigmoid_gate * (1.0 + pre_gate * (1.0 - sigmoid_gate))
            pre[1] = swish_gate
            return

        @pl.when(c == 0)
        def _():
            weight_loads[2].wait()

        project(c, 1, (2,))
        d_hidden = pre[2]
        gate_part = jnp.sum(pre[3] * d_hidden, axis=1, keepdims=True)
        part[c, :, 0:LANES] = jnp.broadcast_to(gate_part, (MANY, LANES)).astype(BF)
        d_gate = (d_hidden * pre[0]).astype(BF)
        d_up = (d_hidden * pre[1]).astype(BF)
        grads[0] = d_gate
        grads[1] = d_up

        def unproject(k, carry):
            at = pl.ds(pl.multiple_of(k * NTILE, NTILE), NTILE)
            to = pl.ds(pl.multiple_of(LANES + k * NTILE, LANES), NTILE)
            part[c, :, to] = (
                jnp.dot(grads[0], wts[0, :, at], preferred_element_type=F32)
                + jnp.dot(grads[1], wts[1, :, at], preferred_element_type=F32)
            ).astype(BF)
            return carry

        quarter = HALF // 2 // NTILE
        for t in range(2):
            for side, kinds in ((0, (0, 3)), (1, (1, 2))):
                first = (2 * t + side) * quarter
                lax.fori_loop(first, first + quarter, unproject, 0)
                for kind in kinds:
                    scatter_copy(c, t, kind).start()

    def scatter_columns(t, side):
        start = LANES + t * HALF + side * HALF // 2
        return (0 if t == 0 and side == 0 else start), start + HALF // 2

    def scatter_copy(c, t, kind):
        p = part.at[c]
        from_left_rows, far, from_right_rows = (pl.ds(i * ROWS, ROWS) for i in (1, 2, 3))
        a, b = (pl.ds(i, j - i) for i, j in (scatter_columns(t, 0), scatter_columns(t, 1)))
        ref_pair, to = (
            ((p.at[far, a], relay.at[c, :, a]), right),
            ((p.at[far, b], relay.at[c, :, b]), left),
            ((p.at[from_right_rows, b], full.at[c, 0, :, b]), right),
            ((p.at[from_left_rows, a], full.at[c, 1, :, a]), left),
            ((p.at[from_right_rows, a], full.at[c, 0, :, a]), right),
            ((p.at[from_left_rows, b], full.at[c, 1, :, b]), left),
        )[kind]
        return pltpu.make_async_remote_copy(
            src_ref=ref_pair[0],
            dst_ref=ref_pair[1],
            send_sem=rs_send.at[c, t, kind],
            recv_sem=rs_recv.at[c, t, kind],
            device_id=to,
            device_id_type=MESH,
        )

    def pass_on(c, t):
        for kind, rows in ((0, slice(3 * ROWS, 4 * ROWS)), (1, slice(ROWS, 2 * ROWS))):
            scatter_copy(c, t, kind).wait_recv()
            cols = slice(*scatter_columns(t, kind))
            part[c, rows, cols] = (
                part[c, rows, cols].astype(F32) + relay[c, :, cols].astype(F32)
            ).astype(BF)
            scatter_copy(c, t, kind + 4).start()

    def send_home(c, t):
        for kind in (2, 3, 4, 5):
            scatter_copy(c, t, kind).wait_recv()

        def total(at):
            return (
                part[c, 0:ROWS, at].astype(F32)
                + full[c, 0, :, at].astype(F32)
                + full[c, 1, :, at].astype(F32)
            ).astype(BF)

        rows = pltpu.einshape(
            "a(bc)->abc", total(slice(LANES + t * HALF, LANES + (t + 1) * HALF)), c=LANES
        )
        ret_out[pl.ds(c * PER, PER), 16 + t * PIECE : 16 + (t + 1) * PIECE, :] = (
            rows.reshape(PER, PIECE, LANES)
        )
        if t == 0:
            r0 = lax.broadcasted_iota(jnp.int32, (PER * 16, ROWS), 0)
            r1 = lax.broadcasted_iota(jnp.int32, (PER * 16, ROWS), 1)
            spread = jnp.where(
                (r1 == (r0 >> 4) * CAP + (r0 & 15)) & ((r0 & 15) < CAP), 1.0, 0.0
            ).astype(BF)
            gates = jnp.dot(spread, total(slice(0, LANES)), preferred_element_type=F32)
            ret_out[pl.ds(c * PER, PER), 0:16, :] = gates.astype(BF).reshape(
                PER, 16, LANES
            )

        def send(k, to):
            pltpu.make_async_remote_copy(
                src_ref=ret_out.at[k, returned(t)],
                dst_ref=ret_in.at[k, returned(t)],
                send_sem=ret_send.at[c, t],
                recv_sem=ret_recv.at[c, t],
                device_id=to,
                device_id_type=MESH,
            ).start()

        each_peer(c * GROUPS // CHUNKS, (c + 1) * GROUPS // CHUNKS, -1, send)

        @pl.when(c == SELF_CHUNK)
        def _():
            ret_in[SELF_CHUNK * PER, returned(t)] = ret_out[SELF_CHUNK * PER, returned(t)]

    def returned(t):
        return pl.ds(0, 16 + PIECE) if t == 0 else pl.ds(16 + PIECE, PIECE)

    def await_return(c, t, sem):
        def wait(at):
            pltpu.make_async_copy(
                ret_out.at[at, returned(t)], ret_in.at[at, returned(t)], sem.at[c, t]
            ).wait()

        @pl.when(c == SELF_CHUNK)
        def _():
            wait(pl.ds(SELF_CHUNK * PER + 1, PER - 1))

        @pl.when(c != SELF_CHUNK)
        def _():
            wait(pl.ds(c * PER, PER))

    def home_copy(c):
        at = pl.ds(c * ROWS, ROWS)
        return pltpu.make_async_copy(home.at[at], home_hbm.at[at], out_sem.at[c])

    def come_home(c):
        for t in range(2):
            await_return(c, t, ret_recv)
            rows = ret_in[pl.ds(c * PER, PER), 16 + t * PIECE : 16 + (t + 1) * PIECE, :]
            home[pl.ds(c * ROWS, ROWS), t * HALF : (t + 1) * HALF] = pltpu.einshape(
                "abc->a(bc)", rows.reshape(ROWS, SUB // 2, LANES)
            )
        home_copy(c).start()

    def finish():
        at = lax.broadcasted_iota(jnp.int32, (TOK, PEERS * 16), 1)
        pick = jnp.where(at == peer_of * 16 + position, 1.0, 0.0).astype(BF)
        gates = jnp.dot(
            pick,
            ret_in[:, 0:16, :].reshape(PEERS * 16, LANES),
            preferred_element_type=F32,
        )
        ggrad = jnp.where(t0 == t1, gates / gate, 0.0)
        ggrad_ref[...] = jnp.sum(ggrad, axis=0, keepdims=True)
        slot_ref[...] = slot_row

    def drain():
        def ended(c, carry):
            for n in range(PIECES):
                await_dispatch(c, n, disp_send)
                for kind in range(4):
                    gather_copy(c, n, kind).wait_send()
            for t in range(2):
                for kind in range(6):
                    scatter_copy(c, t, kind).wait_send()
                await_return(c, t, ret_send)
            home_copy(c).wait()
            return carry

        lax.fori_loop(0, CHUNKS, ended, 0)

    def sd(c, h):
        def piece(n, carry):
            sort(c, n)
            dispatch(c, n)
            return carry

        lax.fori_loop(h * SPLIT, (h + 1) * SPLIT, piece, 0)

    loads[0].wait()
    sort(0, 0)
    pl.semaphore_wait(barrier, PEERS - 1 + 2)
    dispatch(0, 0)
    for n in range(1, SPLIT):
        sort(0, n)
        dispatch(0, n)
    loads[1].wait()
    for j in range(0, D, 1024):
        src[1, :, j : j + 1024] = (gate * src[1, :, j : j + 1024].astype(F32)).astype(BF)
    sd(0, 1)
    arrive(0, 0)
    sd(1, 0)
    sd(1, 1)
    arrive(0, 1)
    sd(2, 0)
    sd(2, 1)
    forward(0, 0)
    sd(3, 0)
    sd(3, 1)

    def step(c, carry):
        @pl.when(c < CHUNKS - 1)
        def _():
            arrive(c + 1, 0)

        forward(c, 1)
        compute(c, 0)

        @pl.when(c > 0)
        def _():
            pass_on(c - 1, 0)
            pass_on(c - 1, 1)

        @pl.when(c < CHUNKS - 1)
        def _():
            arrive(c + 1, 1)
            forward(c + 1, 0)

        compute(c, 1)

        @pl.when(c > 0)
        def _():
            send_home(c - 1, 0)
            send_home(c - 1, 1)

        return carry

    lax.fori_loop(0, CHUNKS, step, 0)
    pass_on(CHUNKS - 1, 0)
    pass_on(CHUNKS - 1, 1)
    lax.fori_loop(0, 2, lambda c, carry: come_home(c) or carry, 0)
    send_home(CHUNKS - 1, 0)
    send_home(CHUNKS - 1, 1)
    lax.fori_loop(2, CHUNKS, lambda c, carry: come_home(c) or carry, 0)
    finish()
    drain()


def unsort(home_ref, gate_ref, slot_ref, dtok_ref, ggrad_ref):
    t0 = lax.broadcasted_iota(jnp.int32, (TOK, TOK), 0)
    t1 = lax.broadcasted_iota(jnp.int32, (TOK, TOK), 1)
    slot = jnp.sum(jnp.where(t0 == t1, slot_ref[...], 0), axis=1, keepdims=True)
    at = lax.broadcasted_iota(jnp.int32, (TOK, SLOTS), 1)
    pick = jnp.where(at == slot, 1.0, 0.0).astype(BF)
    dtok_ref[...] = jnp.dot(pick, home_ref[...], preferred_element_type=F32).astype(BF)
    ggrad_ref[...] = gate_ref[...].astype(BF)


def local(tokens, cotangent, expert_ids, gate_values, gate_weight, up_weight, down_weight):
    vmem = pl.BlockSpec(memory_space=pltpu.VMEM)
    hbm = pl.BlockSpec(memory_space=pl.ANY)
    dma = pltpu.SemaphoreType.DMA
    home, gate_grad, slot = pl.pallas_call(
        kernel,
        out_shape=(
            jax.ShapeDtypeStruct((SLOTS, D), BF),
            jax.ShapeDtypeStruct((1, TOK), F32),
            jax.ShapeDtypeStruct((1, TOK), jnp.int32),
        ),
        in_specs=[hbm, hbm, vmem, vmem, hbm, hbm, hbm],
        out_specs=(hbm, vmem, vmem),
        scratch_shapes=[
            pltpu.VMEM((2, TOK, D), BF),
            pltpu.VMEM((3, HID, D), BF),
            pltpu.VMEM((PIECES, SLOTS, PSUB, LANES), BF),
            pltpu.VMEM((PIECES, SLOTS, PSUB, LANES), BF),
            pltpu.VMEM((2, CHUNKS, MANY, D), BF),
            pltpu.VMEM((4, MANY, HID), F32),
            pltpu.VMEM((2, MANY, HID), BF),
            pltpu.VMEM((CHUNKS, MANY, WIDE), BF),
            pltpu.VMEM((CHUNKS, ROWS, WIDE), BF),
            pltpu.VMEM((CHUNKS, 2, ROWS, WIDE), BF),
            pltpu.VMEM((PEERS, BACK, LANES), BF),
            pltpu.VMEM((PEERS, BACK, LANES), BF),
            pltpu.VMEM((SLOTS, D), BF),
            dma((2,)),
            dma((3,)),
            dma((PIECES, CHUNKS)),
            dma((PIECES, CHUNKS)),
            dma((PIECES, CHUNKS, 4)),
            dma((PIECES, CHUNKS, 4)),
            dma((CHUNKS, 2, 6)),
            dma((CHUNKS, 2, 6)),
            dma((CHUNKS, 2)),
            dma((CHUNKS, 2)),
            dma((CHUNKS,)),
        ],
        compiler_params=pltpu.CompilerParams(
            collective_id=0, has_side_effects=True, vmem_limit_bytes=60 * 2**20
        ),
    )(
        tokens,
        cotangent,
        expert_ids.reshape(1, TOK),
        gate_values.reshape(1, TOK),
        gate_weight,
        up_weight,
        down_weight,
    )
    d_tokens, gate_grad = pl.pallas_call(
        unsort,
        grid=(D // UNSORT,),
        out_shape=(
            jax.ShapeDtypeStruct((TOK, D), BF),
            jax.ShapeDtypeStruct((1, TOK), BF),
        ),
        in_specs=[
            pl.BlockSpec((SLOTS, UNSORT), lambda j: (0, j)),
            pl.BlockSpec((1, TOK), lambda j: (0, 0)),
            pl.BlockSpec((1, TOK), lambda j: (0, 0)),
        ],
        out_specs=(
            pl.BlockSpec((TOK, UNSORT), lambda j: (0, j)),
            pl.BlockSpec((1, TOK), lambda j: (0, 0)),
        ),
    )(home, gate_grad, slot)
    return d_tokens, gate_grad.reshape(TOK, 1)


def solution(mesh):
    rows = P(("expert", "tensor"), None)
    blocks = P(("expert", "tensor"), None, None)
    return jax.shard_map(
        local,
        mesh=mesh,
        in_specs=(rows, rows, rows, rows, blocks, blocks, blocks),
        out_specs=(rows, rows),
        check_vma=False,
    )
```
